32 devices in a mesh: row: 4 (over z), head: 8 (over y, x, core).
Axes of the slice: x: 2, y: 2, z: 4, core: 2. Of those that a mesh axis runs over, the one named last changes fastest.
Arguments:
- hidden: bfloat16 [8, 8192], P(None, 'row'), may hold values from -12 to 12
- norm_gain: bfloat16 [8192], P('row'), may hold values from 0.5 to 1.5
- input_weight: bfloat16 [8192, 2, 16384], P('row', None, 'head'), may hold values from -0.0625 to 0.0625
- group_weight: bfloat16 [8192, 4096], P('row', 'head'), may hold values from -0.0625 to 0.0625
- step_weight: bfloat16 [8192, 256], P('row', 'head'), may hold values from -0.0625 to 0.0625
- conv_inner_weight: bfloat16 [4, 16384], P(None, 'head'), may hold values from -3 to 3
- conv_group_weight: bfloat16 [4, 4096], P(None, 'head'), may hold values from -3 to 3
- conv_inner_state: bfloat16 [8, 3, 16384], P('row', None, 'head'), may hold values from -6 to 6
- conv_group_state: bfloat16 [8, 3, 4096], P('row', None, 'head'), may hold values from -6 to 6
- timestep_bias: float32 [256], P('head'), may hold values from -3 to 0.5
- decay_log: float32 [256], P('head'), may hold values from -1 to 2
- skip_gain: float32 [256], P('head'), may hold values from 0.5 to 1.5
- recurrent_state: bfloat16 [8, 256, 64, 256], P('row', 'head'), may hold values from -6 to 6
- mixer_gain: bfloat16 [16384], P('head'), may hold values from 0.5 to 1.5
- output_weight: bfloat16 [16384, 8192], P('head', 'row'), may hold values from -0.046875 to 0.046875
- final_gain: bfloat16 [8192], P('row'), may hold values from 0.5 to 1.5
- lexicon_matrix: bfloat16 [8192, 65536], P('row', 'head'), may hold values from -0.4375 to 0.4375
- token_mask: int32 [8, 65536], P('row', 'head'), may hold values 0 or 1
- min_share: int32 [8], P('row'), may hold values from 1311 to 13107
Outputs:
- next_state: bfloat16 [8, 256, 64, 256], P('row', 'head')
- next_conv_inner: bfloat16 [8, 3, 16384], P('row', None, 'head')
- next_conv_group: bfloat16 [8, 3, 4096], P('row', None, 'head')
- layer_out: bfloat16 [8, 8192], P(None, 'row')
- next_probs: bfloat16 [8, 65536], P('row', 'head')
The draws below stay inside these ranges and needn't reach their ends.
Inputs may be any that keep to these rules, and one draw needn't show every extreme that they name: `min_share`: the smallest share of the row's top probability that a token keeps in full at twice that share, times 65536.
All inputs are finite; a program needn't handle non-finite values. No bound on the sum of `token_mask` on one device may be relied on, other than what follows from the above.
Results may differ from the reference program's by a relative error of at most 0.04.
Values may be sent and summed in bfloat16 or wider, within the bound.
No kernel may reach another device: no remote copies, remote signals or barrier semaphores. Data moves between devices by JAX's collectives and lax.ppermute only.
A program may use at most 128 MiB of HBM per device.

```python
import math
import jax
import jax.numpy as jnp
from jax import lax

D = 8192
HEADS = 256
HEAD_DIM = 64
STATE = 256
GROUPS = 8
VOCAB = 65536
CONV = 4
ROWS = 8


def draw_hidden(key, part):
    key_list = jax.random.split(jax.random.fold_in(key, 17), 3)
    base_draw = jax.random.normal(key_list[0], (ROWS, D), jnp.float32)
    row_scale = jnp.exp(jax.random.uniform(key_list[1], (ROWS, 1), jnp.float32, math.log(0.3), math.log(3.0)))
    column_ramp = jnp.exp(math.log(3.0) * jnp.arange(D, dtype=jnp.float32)[None, :] / D)
    column_scale = 0.6 * column_ramp * jnp.exp(jax.random.uniform(key_list[2], (1, D), jnp.float32, -0.7, 0.7))
    return jnp.clip(base_draw * row_scale * column_scale, -12.0, 12.0).astype(jnp.bfloat16)


def plant(values, key, least, largest):
    place = [jax.random.randint(jax.random.fold_in(key, axis), (), 0, length) for axis, length in enumerate(values.shape)]
    longest = values.shape.index(max(values.shape))
    next_to = place[:longest] + [(place[longest] + 1) % values.shape[longest]] + place[longest + 1:]
    return values.at[tuple(place)].set(least).at[tuple(next_to)].set(largest)


def levels(own_key, shape, cuts, smallest, high):
    loudness = 1.0
    for axis_at, parts in cuts:
        heights = jax.random.uniform(jax.random.fold_in(jax.random.fold_in(own_key, 6), axis_at), (parts,), jnp.float32, smallest / len(cuts), high / len(cuts))
        loudness = loudness * jnp.repeat(jnp.exp(heights), shape[axis_at] // parts).reshape((-1,) + (1,) * (len(shape) - 1 - axis_at))
    return loudness


def centred(own_key, dims, spread, limit, cuts=(), kind=jnp.bfloat16):
    array = spread * jax.random.normal(own_key, dims, jnp.float32)
    if cuts:
        array = array * levels(own_key, dims, cuts, -0.22, 0.18)
    return jnp.clip(array, -limit, limit).astype(kind)


def setup_inputs(seed: int = 0) -> dict:
    keys = jax.random.split(jax.random.key(seed), 20)
    return {
        "hidden": draw_hidden(jax.random.fold_in(keys[19], 71), 0),
        "norm_gain": jnp.clip(1.0 + 0.1 * jax.random.normal(keys[1], (D,), jnp.float32), 0.5, 1.5).astype(jnp.bfloat16),
        "input_weight": centred(keys[2], (D, 2, HEADS * HEAD_DIM), D ** -0.5, 0.0625, ((0, 4), (2, 8))),
        "group_weight": centred(keys[3], (D, GROUPS * 2 * STATE), D ** -0.5, 0.0625, ((0, 4), (1, 8))),
        "step_weight": centred(keys[4], (D, HEADS), D ** -0.5, 0.0625, ((0, 4), (1, 8))),
        "conv_inner_weight": centred(keys[5], (CONV, HEADS * HEAD_DIM), 0.5, 3.0, ((1, 8),)),
        "conv_group_weight": centred(keys[6], (CONV, GROUPS * 2 * STATE), 0.5, 3.0, ((1, 8),)),
        "conv_inner_state": centred(keys[7], (ROWS, CONV - 1, HEADS * HEAD_DIM), 1.0, 6.0, ((0, 4), (2, 8))),
        "conv_group_state": centred(keys[8], (ROWS, CONV - 1, GROUPS * 2 * STATE), 1.0, 6.0, ((0, 4), (2, 8))),
        "timestep_bias": jnp.clip(-3.0 + 3.5 * jax.random.uniform(keys[9], (HEADS,), jnp.float32) ** levels(keys[9], (HEADS,), ((0, 8),), -0.2, 0.2), -3.0, 0.5),
        "decay_log": jnp.clip(-1.0 + 3.0 * jax.random.uniform(keys[10], (HEADS,), jnp.float32) ** levels(keys[10], (HEADS,), ((0, 8),), -0.2, 0.2), -1.0, 2.0),
        "skip_gain": jnp.clip(0.5 + 1.0 * jax.random.uniform(keys[11], (HEADS,), jnp.float32) ** levels(keys[11], (HEADS,), ((0, 8),), -0.2, 0.2), 0.5, 1.5),
        "recurrent_state": centred(keys[12], (ROWS, HEADS, HEAD_DIM, STATE), 1.0, 6.0, ((0, 4), (1, 8))),
        "mixer_gain": jnp.clip(1.0 + 0.1 * jax.random.normal(keys[13], (HEADS * HEAD_DIM,), jnp.float32), 0.5, 1.5).astype(jnp.bfloat16),
        "output_weight": centred(keys[14], (HEADS * HEAD_DIM, D), (HEADS * HEAD_DIM) ** -0.5, 0.046875, ((0, 8), (1, 4))),
        "final_gain": jnp.clip(1.0 + 0.1 * jax.random.normal(keys[15], (D,), jnp.float32), 0.5, 1.5).astype(jnp.bfloat16),
        "lexicon_matrix": centred(keys[16], (D, VOCAB), (2.5 * D ** -0.5), 0.4375, ((0, 4), (1, 8))),
        "token_mask": plant((jax.random.randint(keys[17], (ROWS, VOCAB), 0, 10) < 9).astype(jnp.int32), jax.random.fold_in(keys[17], 1), 0, 1),
        "min_share": plant(jax.random.randint(keys[18], (ROWS,), 1311, 13108), jax.random.fold_in(keys[18], 1), 1311, 13107).astype(jnp.int32),
    }


EPSILON = 1e-05
INVERSE_HEAT = 1.25
FIXED_POINT = 65536.0
NEG_LARGE = -1e+30

def conv_step(history, newest, filter_coefficient):
    window = jnp.concatenate([history, newest[:, None, :]], axis=1)
    mixed_taps = lax.optimization_barrier(jnp.sum(window.astype(jnp.float32) * filter_coefficient.astype(jnp.float32)[None, :, :], axis=1))
    return (window[:, 1:, :], jax.nn.silu(mixed_taps))

def leading(values_in):
    return jnp.moveaxis(values_in, 1, 0)

def one_group(items):
    state_old, inner_part, pair_part, steps, decays = items
    state_new = decays[:, :, None, None] * state_old.astype(jnp.float32) + (steps[:, :, None] * inner_part)[:, :, :, None] * pair_part[:, None, None, 0, :]
    readout = lax.optimization_barrier(jnp.sum(state_new * pair_part[:, None, None, 1, :], axis=3))
    return (state_new.astype(jnp.bfloat16), readout)

def reference(hidden, norm_gain, input_weight, group_weight, step_weight, conv_inner_weight, conv_group_weight, conv_inner_state, conv_group_state, timestep_bias, decay_log, skip_gain, recurrent_state, mixer_gain, output_weight, final_gain, lexicon_matrix, token_mask, min_share):
    hidden_wide = hidden.astype(jnp.float32)
    hidden_scale = lax.rsqrt(lax.optimization_barrier(jnp.mean(hidden_wide * hidden_wide, axis=1, keepdims=True)) + EPSILON)
    normed = (hidden_wide * hidden_scale * norm_gain.astype(jnp.float32)[None, :]).astype(jnp.bfloat16)
    gate_raw = jnp.dot(normed, input_weight[:, 0, :], preferred_element_type=jnp.float32)
    inner_raw = jnp.dot(normed, input_weight[:, 1, :], preferred_element_type=jnp.float32)
    group_raw = jnp.dot(normed, group_weight, preferred_element_type=jnp.float32)
    step_raw = jnp.dot(normed, step_weight, preferred_element_type=jnp.float32)
    next_conv_inner, conv_inner = conv_step(conv_inner_state, inner_raw.astype(jnp.bfloat16), conv_inner_weight)
    next_conv_group, conv_group = conv_step(conv_group_state, group_raw.astype(jnp.bfloat16), conv_group_weight)
    group_round = lax.optimization_barrier(conv_group.astype(jnp.bfloat16)).astype(jnp.float32)
    step_size = jax.nn.softplus(step_raw + timestep_bias[None, :])
    decay_rate = jnp.exp(-step_size * jnp.exp(decay_log)[None, :])
    heads_group = HEADS // GROUPS
    pair_groups = jnp.transpose(group_round.reshape(ROWS, 2, STATE, GROUPS), (0, 3, 1, 2))
    inner_groups = conv_inner.reshape(ROWS, GROUPS, heads_group, HEAD_DIM)
    state_groups = recurrent_state.reshape(ROWS, GROUPS, heads_group, HEAD_DIM, STATE)
    step_groups = step_size.reshape(ROWS, GROUPS, heads_group)
    decay_groups = decay_rate.reshape(ROWS, GROUPS, heads_group)
    states_new, readout = lax.map(one_group, (leading(state_groups), leading(inner_groups), leading(pair_groups), leading(step_groups), leading(decay_groups)))
    next_state = jnp.moveaxis(states_new, 0, 1).reshape(ROWS, HEADS, HEAD_DIM, STATE)
    readout = jnp.moveaxis(readout, 0, 1).reshape(ROWS, HEADS, HEAD_DIM)
    readout = readout + skip_gain[None, :, None] * conv_inner.reshape(ROWS, HEADS, HEAD_DIM)
    gated_out = readout.reshape(ROWS, HEADS * HEAD_DIM) * jax.nn.silu(gate_raw)
    gated_groups = gated_out.reshape(ROWS, GROUPS, HEADS * HEAD_DIM // GROUPS)
    group_total = lax.optimization_barrier(jnp.sum(gated_groups * gated_groups, axis=2, keepdims=True))
    group_scale = lax.rsqrt(group_total / (HEADS * HEAD_DIM // GROUPS) + EPSILON)
    mixer_in = ((gated_groups * group_scale).reshape(ROWS, HEADS * HEAD_DIM) * mixer_gain.astype(jnp.float32)[None, :]).astype(jnp.bfloat16)
    mixed = jnp.dot(mixer_in, output_weight, preferred_element_type=jnp.float32)
    layer_out = (hidden_wide + mixed).astype(jnp.bfloat16)
    out_wide = layer_out.astype(jnp.float32)
    out_scale = lax.rsqrt(lax.optimization_barrier(jnp.mean(out_wide * out_wide, axis=1, keepdims=True)) + EPSILON)
    last_rescaled_vector = (out_wide * out_scale * final_gain.astype(jnp.float32)[None, :]).astype(jnp.bfloat16)
    candidate_scores = jnp.dot(last_rescaled_vector, lexicon_matrix, preferred_element_type=jnp.float32) * INVERSE_HEAT
    allowed = token_mask > 0
    peak_logit = lax.optimization_barrier(jnp.max(jnp.where(allowed, candidate_scores, NEG_LARGE), axis=1, keepdims=True))
    ratio_to_peak = jnp.where(allowed, jnp.exp(candidate_scores - peak_logit), 0.0)
    floor_share = min_share.astype(jnp.float32)[:, None] / FIXED_POINT
    weights = ratio_to_peak * jnp.clip(ratio_to_peak / floor_share - 1.0, 0.0, 1.0)
    kept_total = lax.optimization_barrier(jnp.sum(weights, axis=1, keepdims=True))
    next_probs = (weights / kept_total).astype(jnp.bfloat16)
    return (next_state, next_conv_inner, next_conv_group, layer_out, next_probs)
```

```python
import functools

import jax
import jax.numpy as jnp
from jax import lax
from jax.experimental import pallas as pl
from jax.experimental.pallas import tpu as pltpu
from jax.sharding import PartitionSpec as P

D = 8192
HEADS = 256
HEAD_DIM = 64
GROUPS = 8

EPSILON = 1e-05
INVERSE_HEAT = 1.25
FIXED_POINT = 65536.0
NEG_LARGE = -1e30

MIB = 2**20
LANES = 128
TILE = 256
SHARES = (3, 12, 18, 24)
VMEM = pl.BlockSpec(memory_space=pltpu.VMEM)
ANY = pl.BlockSpec(memory_space=pl.ANY)
f32 = jnp.float32
bf16 = jnp.bfloat16


def xor_permute(values, axis, distance):
    size = lax.axis_size(axis)
    return lax.ppermute(values, axis, [(at, at ^ distance) for at in range(size)])


def tree_sum(values):
    values = list(values)
    while len(values) > 1:
        values = [a + b for a, b in zip(values[0::2], values[1::2])]
    return values[0]


def split(values):
    high = values.astype(bf16)
    return high, (values - high.astype(f32)).astype(bf16)


def split_three(values):
    high, rest = split(values)
    middle = values - high.astype(f32)
    return high, rest, (middle - rest.astype(f32)).astype(bf16)


def silu(values):
    return values / (1.0 + jnp.exp(-values))


def dot(left, right):
    return jnp.dot(left, right, preferred_element_type=f32)


def dot_transposed(left, right):
    return lax.dot_general(left, right, (((1,), (1,)), ((), ())), preferred_element_type=f32)


def in_hbm(values):
    return pltpu.with_memory_space_constraint(values, pltpu.HBM)


def call(kernel, outs, operands, specs, scratch=(), limit=4, cost=0, out_specs=None, name=None):
    return pl.pallas_call(
        kernel,
        out_shape=outs,
        in_specs=specs,
        out_specs=out_specs if out_specs is not None else jax.tree.map(lambda _: VMEM, outs),
        scratch_shapes=list(scratch),
        compiler_params=pltpu.CompilerParams(vmem_limit_bytes=limit * MIB),
        cost_estimate=pl.CostEstimate(flops=1000, bytes_accessed=cost, transcendentals=0),
        name=name,
    )(*operands)


def shape(dims, dtype=f32):
    return jax.ShapeDtypeStruct(tuple(dims), dtype)


def squares_kernel(count, *refs):
    sources, targets = refs[:count], refs[count : 2 * count]
    squares_ref, sems = refs[2 * count :]
    copies = [pltpu.make_async_copy(sources[at], targets[at], sems.at[at]) for at in range(count)]
    for copy in copies:
        copy.start()
    for copy in copies:
        copy.wait()
    wide = targets[0][...].astype(f32)
    squares_ref[...] = jnp.broadcast_to(jnp.sum(wide * wide, axis=1, keepdims=True), squares_ref.shape)


def prepare_kernel(pieces, *refs):
    hidden_ref, gain_ref, step_ref, state_ref, taps_ref, weight_ref = refs[pieces : pieces + 6]
    normed_ref, sent_ref, small_ref, stack = refs[pieces + 6 :]
    rows = hidden_ref.shape[0]
    columns = weight_ref.shape[1]
    entries = columns // GROUPS
    devices = sent_ref.shape[0]
    squares = tree_sum([ref[...] for ref in refs[:pieces]])[:, 0:1]
    scaled = hidden_ref[...].astype(f32) * lax.rsqrt(squares / D + EPSILON)
    normed = (scaled * gain_ref[...].astype(f32)).astype(bf16)
    normed_ref[...] = normed
    part = dot(normed, weight_ref[...])
    step = dot_transposed(normed, step_ref[...])
    small_ref[:, :columns] = part
    small_ref[:, columns:] = jnp.zeros((rows, LANES), f32)
    small_ref[:, columns : columns + step.shape[1]] = step

    part_high, part_low = split(part)
    stack[...] = jnp.zeros_like(stack)
    stack[:rows] = part_high.astype(f32)
    stack[rows : 2 * rows] = part_low.astype(f32)
    for at in range(3):
        here = 2 * rows + at * state_ref.shape[1]
        stack[here : here + state_ref.shape[1]] = state_ref[at].astype(f32)
    tail = sent_ref.shape[1] - rows
    stack[2 * rows + tail : 2 * rows + tail + taps_ref.shape[0]] = taps_ref[...].astype(f32)
    source = lax.broadcasted_iota(jnp.int32, (columns, columns), 0)
    target = lax.broadcasted_iota(jnp.int32, (columns, columns), 1)
    order = (source % GROUPS) * entries + source // GROUPS == target
    grouped = dot(stack[...].astype(bf16), order.astype(f32).astype(bf16))
    for device in range(devices):
        group = device // (devices // GROUPS)
        here = grouped[:, group * entries : (group + 1) * entries].astype(bf16)
        sent_ref[device, :rows, :entries] = here[:rows]
        sent_ref[device, :rows, entries:] = here[rows : 2 * rows]
        sent_ref[device, rows:, :entries] = here[2 * rows : 2 * rows + tail]
        sent_ref[device, rows:, entries:] = here[2 * rows + tail :]


def input_kernel(normed_ref, weight_ref, _, out_ref, left, held, sems):
    depth, _, width = weight_ref.shape
    rows = normed_ref.shape[0]
    chunks = sems.shape[0]
    part = depth // chunks

    def copy(at):
        here = pl.ds(at * part, part)
        return pltpu.make_async_copy(weight_ref.at[here], held.at[here], sems.at[at])

    for at in range(chunks):
        copy(at).start()
    source = lax.broadcasted_iota(jnp.int32, (LANES, 2 * LANES), 0)
    target = lax.broadcasted_iota(jnp.int32, (LANES, 2 * LANES), 1)
    spread = [(2 * source + at == target).astype(f32).astype(bf16) for at in range(2)]
    for block in range(depth // LANES):
        here = normed_ref[:, block * LANES : (block + 1) * LANES]
        left[:, 2 * block * LANES : 2 * (block + 1) * LANES] = jnp.concatenate(
            [dot(here, spread[at]) for at in range(2)], axis=0
        ).astype(bf16)
    for at in range(chunks):
        copy(at).wait()
        piece = left[:, at * 2 * part : (at + 1) * 2 * part]
        for column in range(0, width, TILE):
            tile = jnp.concatenate(
                [
                    held[at * part : (at + 1) * part, :, start : start + LANES].reshape(2 * part, LANES)
                    for start in range(column, column + TILE, LANES)
                ],
                axis=1,
            )
            term = dot(piece, tile)
            if at == 0:
                out_ref[:, column : column + TILE] = term
            else:
                out_ref[:, column : column + TILE] += term


def pack_kernel(both_ref, small_ref, arrived_ref, out_ref, held_ref):
    rows, width = small_ref.shape[0], both_ref.shape[1]
    blocks, mine, _ = out_ref.shape
    devices, _, double = arrived_ref.shape
    entries = double // 2
    columns = small_ref.shape[1] - LANES
    index = lax.axis_index("row")
    arrived = arrived_ref[...].astype(f32)
    pair = arrived[:, :rows, :entries] + arrived[:, :rows, entries:]
    for device in range(devices):
        here = slice(device * entries, (device + 1) * entries)
        held_ref[0, :, here] = arrived[device, rows:, :entries]
        held_ref[1, :, here] = arrived[device, rows:, entries:]
    for block in range(blocks):
        place = block ^ index
        here = slice(block * mine, (block + 1) * mine)
        out_ref[place, :, :width] = both_ref[here]
        out_ref[place, :, width : 2 * width] = both_ref[rows + block * mine : rows + (block + 1) * mine]
        out_ref[place, :, 2 * width : 2 * width + columns + LANES] = small_ref[here]
        start = 2 * width + columns + LANES
        for device in range(devices):
            out_ref[place, :, start + device * entries : start + (device + 1) * entries] = pair[device, here]


def state_kernel(finish, pieces, *refs):
    parts = [ref[...] for ref in refs[:pieces]]
    (heads_ref, held_ref, inner_state_ref, group_state_ref, inner_taps_ref, group_taps_ref) = refs[
        pieces : pieces + 6
    ]
    del group_taps_ref
    state_ref, gain_ref = refs[pieces + 6 : pieces + 8]
    mixer_ref, next_inner_ref, next_group_ref, driven_ref, decay_ref, input_ref = refs[pieces + 8 :]
    total = tree_sum(parts)
    mine, width, state_width = state_ref.shape
    columns = group_state_ref.shape[2]
    start = 2 * width + columns
    gate = total[:, :width]
    inner_raw = total[:, width : 2 * width].astype(bf16)
    next_inner_ref[0] = inner_state_ref[1]
    next_inner_ref[1] = inner_state_ref[2]
    next_inner_ref[2] = inner_raw
    next_group_ref[0] = group_state_ref[1]
    next_group_ref[1] = group_state_ref[2]
    next_group_ref[2] = total[:, 2 * width : start].astype(bf16)
    taps = inner_taps_ref[...].astype(f32)
    mixed = inner_raw.astype(f32) * taps[3:4]
    for at in range(3):
        mixed = mixed + inner_state_ref[at].astype(f32) * taps[at : at + 1]
    conv_inner = silu(mixed)
    taps = held_ref[1]
    mixed = total[:, start + LANES :].astype(bf16).astype(f32) * taps[3:4]
    for at in range(3):
        mixed = mixed + held_ref[0, at * mine : (at + 1) * mine] * taps[at : at + 1]
    pair = silu(mixed).astype(bf16)
    state_input = pair[:, :state_width].astype(f32)
    state_output = pair[:, state_width:]

    step_raw = total[:, start : start + LANES] + heads_ref[0:1]
    step_size = jnp.maximum(step_raw, 0.0) + jnp.log1p(jnp.exp(-jnp.abs(step_raw)))
    decay_rate = jnp.exp(-step_size * jnp.exp(heads_ref[1:2]))
    stacked = jnp.concatenate([step_size, decay_rate, heads_ref[2:3]], axis=0)
    head = lax.broadcasted_iota(jnp.int32, (LANES, width), 0)
    channel = lax.broadcasted_iota(jnp.int32, (LANES, width), 1)
    spread = (channel // HEAD_DIM == head).astype(f32).astype(bf16)
    wide = tree_sum([dot(part, spread) for part in split_three(stacked)[:2]]) + dot(
        split_three(stacked)[2], spread
    )
    step_wide, decay_wide, skip_wide = wide[:mine], wide[mine : 2 * mine], wide[2 * mine :]
    driven = step_wide * conv_inner
    overlap = jnp.sum(state_input * state_output.astype(f32), axis=1, keepdims=True)
    old = jnp.concatenate(
        [dot_transposed(state_output, state_ref[row])[row : row + 1] for row in range(mine)], axis=0
    )
    readout = decay_wide * old + driven * overlap + skip_wide * conv_inner
    gated = readout * silu(gate)
    driven_ref[...] = driven
    decay_ref[...] = decay_wide
    input_ref[...] = state_input
    if finish:
        group_total = jnp.sum(gated * gated, axis=1, keepdims=True)
        group_scale = lax.rsqrt(group_total / (HEADS * HEAD_DIM // GROUPS) + EPSILON)
        gated = gated * group_scale * gain_ref[...].astype(f32)
    mixer_ref[...] = gated.astype(mixer_ref.dtype)


def update_kernel(driven_ref, decay_ref, input_ref, state_ref, _, out_ref, new, sems):
    mine, width, _ = state_ref.shape
    block = min(512, width)
    blocks = width // block

    def copy(row, at):
        here = pl.ds(at * block, block)
        return pltpu.make_async_copy(new.at[row, here], out_ref.at[row, here], sems.at[row, at])

    for row in range(mine):
        both = jnp.concatenate(
            [driven_ref[row : row + 1], decay_ref[row : row + 1], jnp.zeros((6, width), f32)], axis=0
        )
        turned = jnp.transpose(both)
        for at in range(blocks):
            here = slice(at * block, (at + 1) * block)
            new[row, here] = (
                turned[here, 1:2] * state_ref[row, here].astype(f32)
                + turned[here, 0:1] * input_ref[row : row + 1]
            ).astype(bf16)
            copy(row, at).start()
    for row in range(mine):
        for at in range(blocks):
            copy(row, at).wait()


def output_kernel(pieces, *refs):
    weight_ref, _, out_ref, rows_held = refs[pieces:]
    index = lax.axis_index("row")
    for at in range(pieces):
        rows_held[index ^ at] = refs[at][...].astype(f32)
    left = jnp.concatenate([rows_held[at] for at in range(pieces)], axis=0).astype(bf16)
    width = weight_ref.shape[1]
    for column in range(0, width, TILE):
        out_ref[:, column : column + TILE] = dot(left, weight_ref[:, column : column + TILE])


def add_kernel(left_ref, right_ref, _, out_ref):
    out_ref[...] = left_ref[...] + right_ref[...]


def lexicon_kernel(pieces, *refs):
    hidden_ref, gain_ref, mixed_ref = refs[:3]
    held_refs = refs[3 : 3 + pieces]
    weight_ref, layer_ref, out_ref, rest, left, sems = refs[3 + pieces :]
    rows = hidden_ref.shape[0]
    blocks, mine, _ = out_ref.shape
    vocab = weight_ref.shape[1]
    done = vocab - rest.shape[1]
    copy = pltpu.make_async_copy(weight_ref.at[:, pl.ds(done, vocab - done)], rest, sems.at[0])
    copy.start()
    index = lax.axis_index("row")
    layer = (hidden_ref[...].astype(f32) + mixed_ref[...]).astype(bf16)
    layer_ref[...] = layer
    wide = layer.astype(f32)
    squares = jnp.sum(wide * wide, axis=1, keepdims=True)
    high, low = split(wide * gain_ref[...].astype(f32))
    left[:rows] = high
    left[rows:] = low

    def put(value, column, width):
        for block in range(blocks):
            out_ref[block ^ index, :, column : column + width] = value[block * mine : (block + 1) * mine]

    put(jnp.broadcast_to(squares, (rows, LANES)), vocab, LANES)
    base = 0
    for number, held in enumerate(list(held_refs) + [rest]):
        if number == pieces:
            copy.wait()
        for column in range(0, held.shape[1], TILE):
            term = dot(left[...], held[:, column : column + TILE])
            put(term[:rows] + term[rows:], base + column, TILE)
        base += held.shape[1]


def share_kernel(pieces, *refs):
    mask_ref, sent_ref, share_ref, top_ref, spread = refs[pieces:]
    mine, vocab = mask_ref.shape
    lines = sent_ref.shape[0] // mine
    part = vocab // lines
    total = tree_sum([ref[...] for ref in refs[:pieces]])
    scale = lax.rsqrt(total[:, vocab : vocab + 1] / D + EPSILON) * INVERSE_HEAT
    allowed = mask_ref[...] > 0
    logits = jnp.where(allowed, total[:, :vocab] * scale, NEG_LARGE)
    top = jnp.max(logits, axis=1, keepdims=True)
    share = jnp.where(allowed, jnp.exp(logits - top), 0.0)
    share_ref[...] = share
    top_ref[...] = jnp.broadcast_to(top, top_ref.shape)
    spread[...] = jnp.zeros_like(spread)
    parts = [value.astype(f32) for value in split_three(top)]
    for row in range(mine):
        for line in range(lines):
            here = slice(row * lines + line, row * lines + line + 1)
            spread[here, :part] = share[row : row + 1, line * part : (line + 1) * part]
        here = slice(row * lines, (row + 1) * lines)
        for at in range(3):
            spread[here, part + at : part + at + 1] = jnp.broadcast_to(parts[at][row : row + 1], (lines, 1))
    sent_ref[...] = spread[...].astype(bf16)


def weigh(relative, inverse_floor):
    return relative * jnp.clip(relative * inverse_floor - 1.0, 0.0, 1.0)


def probability_kernel(every_ref, share_ref, top_ref, floor_ref, out_ref):
    mine, vocab = share_ref.shape
    devices, lines, _ = every_ref.shape
    part = vocab * mine // lines
    inverse = FIXED_POINT / floor_ref[:, 0:1].astype(f32)
    tops = [
        jnp.sum(every_ref[device, :, part:].astype(f32), axis=1, keepdims=True)
        for device in range(devices)
    ]
    peak = functools.reduce(jnp.maximum, tops)
    per_row = lines // mine
    spread = jnp.concatenate(
        [jnp.broadcast_to(inverse[row : row + 1], (per_row, 1)) for row in range(mine)], axis=0
    )
    kept = jnp.zeros((lines, part), f32)
    for device in range(devices):
        relative = every_ref[device, :, :part].astype(f32) * jnp.exp(tops[device] - peak)
        kept = kept + weigh(relative, spread)
    kept = jnp.sum(kept, axis=1, keepdims=True)
    total = jnp.concatenate(
        [jnp.sum(kept[row * per_row : (row + 1) * per_row], axis=0, keepdims=True) for row in range(mine)],
        axis=0,
    )
    highest = jnp.concatenate([peak[row * per_row : row * per_row + 1] for row in range(mine)], axis=0)
    own = weigh(share_ref[...] * jnp.exp(top_ref[:, 0:1] - highest), inverse)
    out_ref[...] = (own / total).astype(bf16)


def fetch_kernel(count, starts, *refs):
    sources = refs[:count]
    targets = refs[-count - 1 : -1]
    sems = refs[-1]
    copies = []
    for at in range(count):
        source = sources[at]
        if starts[at] is not None:
            source = source.at[:, pl.ds(starts[at], targets[at].shape[1])]
        copies.append(pltpu.make_async_copy(source, targets[at], sems.at[at]))
    for copy in copies:
        copy.start()
    for copy in copies:
        copy.wait()


def fetch(sources, columns, after, name):
    outs = []
    size = 0
    for source, part in zip(sources, columns):
        dims = source.shape if part is None else (source.shape[0], part[1])
        outs.append(pltpu.VMEM(dims, source.dtype))
        size += 2 * functools.reduce(lambda a, b: a * b, dims)
    starts = [None if part is None else part[0] for part in columns]
    return call(
        functools.partial(fetch_kernel, len(sources), starts),
        outs,
        [in_hbm(source) for source in sources] + [after],
        [ANY] * (len(sources) + 1),
        scratch=[pltpu.SemaphoreType.DMA((len(sources),))],
        limit=1,
        cost=size,
        out_specs=[VMEM] * len(outs),
        name=name,
    )


def local(
    hidden,
    norm_gain,
    input_weight,
    group_weight,
    step_weight,
    conv_inner_weight,
    conv_group_weight,
    conv_inner_state,
    conv_group_state,
    timestep_bias,
    decay_log,
    skip_gain,
    recurrent_state,
    mixer_gain,
    output_weight,
    final_gain,
    lexicon_matrix,
    token_mask,
    min_share,
):
    mine, heads_mine, head_width, state_width = recurrent_state.shape
    width = heads_mine * head_width
    rows, depth = hidden.shape
    vocab = lexicon_matrix.shape[1]
    row_devices = lax.axis_size("row")
    head_devices = lax.axis_size("head")
    group_devices = head_devices // GROUPS
    columns = group_weight.shape[1]
    entries = columns // GROUPS
    held_rows = -(-3 * mine // 8) * 8

    heads = jnp.pad(
        jnp.stack([timestep_bias, decay_log, skip_gain]), ((0, 0), (0, LANES - heads_mine))
    )
    inner_state = jnp.moveaxis(conv_inner_state, 1, 0)
    group_state = jnp.moveaxis(conv_group_state, 1, 0)
    state = recurrent_state.reshape(mine, width, state_width)
    floors = jnp.broadcast_to(min_share[:, None], (mine, LANES))

    small_arrays = [hidden, norm_gain[None], step_weight.T, group_state, conv_group_weight]
    *small_held, squares = call(
        functools.partial(squares_kernel, len(small_arrays)),
        [pltpu.VMEM(array.shape, array.dtype) for array in small_arrays] + [shape((rows, LANES))],
        [in_hbm(array) for array in small_arrays],
        [ANY] * len(small_arrays),
        scratch=[pltpu.SemaphoreType.DMA((len(small_arrays),))],
        limit=1,
        out_specs=[VMEM] * (len(small_arrays) + 1),
        name="squares",
    )
    all_squares = [squares] + [xor_permute(squares, "row", at) for at in range(1, row_devices)]
    (group_held,) = fetch([group_weight], [None], squares, "fetch_group")
    normed, sent, small = call(
        functools.partial(prepare_kernel, row_devices),
        [
            shape((rows, depth), bf16),
            shape((head_devices, rows + held_rows, 2 * entries), bf16),
            shape((rows, columns + LANES)),
        ],
        all_squares + small_held + [group_held],
        [VMEM] * (row_devices + 6),
        scratch=[pltpu.VMEM((2 * rows + 2 * held_rows, columns), f32)],
        limit=4,
        cost=2 * MIB,
        name="group_projection",
    )
    arrived = lax.all_to_all(sent, "head", 0, 0, tiled=True)

    chunks = 8
    both = call(
        input_kernel,
        shape((2 * rows, width)),
        [normed, in_hbm(input_weight), sent],
        [VMEM, ANY, ANY],
        scratch=[
            pltpu.VMEM((2 * rows, 2 * depth), bf16),
            pltpu.VMEM((depth, 2, width), bf16),
            pltpu.SemaphoreType.DMA((chunks,)),
        ],
        limit=24,
        cost=2 * input_weight.size,
        name="input_projection",
    )
    packed_width = 2 * width + columns + LANES + 2 * state_width
    packed, held = call(
        pack_kernel,
        [shape((row_devices, mine, packed_width)), shape((2, held_rows, 2 * state_width))],
        [both, small, arrived],
        [VMEM] * 3,
        name="pack_rows",
    )
    pieces = [packed[0]] + [xor_permute(packed[at], "row", at) for at in range(1, row_devices)]

    tiles = vocab // TILE
    cuts = [tiles * share // 32 * TILE for share in SHARES]
    spans = [(start, end - start) for start, end in zip([0] + cuts[:-1], cuts)]
    fetched = []

    def fetch_lexicon(stage, after, name):
        if spans[stage][1]:
            fetched.extend(fetch([lexicon_matrix], [spans[stage]], after, name))
            return fetched[-1]
        return after

    output_held, state_held, *fetched = fetch(
        [output_weight, state] + [lexicon_matrix] * (spans[0][1] > 0),
        [None, None] + [spans[0]] * (spans[0][1] > 0),
        packed,
        "fetch_output",
    )

    finish = group_devices == 1
    mixer_in, next_inner, next_group, driven, decay, state_input = call(
        functools.partial(state_kernel, finish, row_devices),
        [
            shape((mine, width), bf16 if finish else f32),
            shape((3, mine, width), bf16),
            shape((3, mine, columns), bf16),
            shape((mine, width)),
            shape((mine, width)),
            shape((mine, state_width)),
        ],
        pieces
        + [heads, held, inner_state, group_state, conv_inner_weight, conv_group_weight, state_held]
        + [mixer_gain[None]],
        [VMEM] * (row_devices + 8),
        limit=8,
        cost=2 * MIB,
        name="state_readout",
    )
    if not finish:
        members = [
            [group * group_devices + at for at in range(group_devices)] for group in range(GROUPS)
        ]
        group_total = lax.psum(jnp.sum(mixer_in * mixer_in, axis=1), "head", axis_index_groups=members)
        group_scale = lax.rsqrt(group_total / (HEADS * HEAD_DIM // GROUPS) + EPSILON)
        mixer_in = (mixer_in * group_scale[:, None] * mixer_gain.astype(f32)[None]).astype(bf16)

    mixer_rows = [mixer_in] + [xor_permute(mixer_in, "row", at) for at in range(1, row_devices)]
    ahead = fetch_lexicon(1, mixer_in, "fetch_lexicon_1")
    mixed = call(
        functools.partial(output_kernel, row_devices),
        shape((rows, depth)),
        mixer_rows + [output_held, ahead],
        [VMEM] * (row_devices + 1) + [ANY],
        scratch=[pltpu.VMEM((row_devices, mine, width), f32)],
        cost=4 * MIB,
        name="output_projection",
    )
    distance = 1
    while distance < head_devices:
        other = xor_permute(mixed, "head", distance)
        ahead = mixed
        for stage, place in ((2, head_devices // 4), (3, head_devices // 2)):
            if distance == place:
                ahead = fetch_lexicon(stage, mixed, f"fetch_lexicon_{stage}")
        mixed = call(
            add_kernel, shape((rows, depth)), [mixed, other, ahead], [VMEM, VMEM, ANY], name="add"
        )
        distance *= 2
    layer_out, scores = call(
        functools.partial(lexicon_kernel, len(fetched)),
        [shape((rows, depth), bf16), shape((row_devices, mine, vocab + LANES))],
        [hidden, final_gain[None], mixed] + fetched + [in_hbm(lexicon_matrix)],
        [VMEM] * (3 + len(fetched)) + [ANY],
        scratch=[
            pltpu.VMEM((depth, vocab - cuts[-1]), bf16),
            pltpu.VMEM((2 * rows, depth), bf16),
            pltpu.SemaphoreType.DMA((1,)),
        ],
        limit=12,
        cost=16 * MIB,
        name="lexicon_projection",
    )
    score_rows = [scores[0]] + [xor_permute(scores[at], "row", at) for at in range(1, row_devices)]
    next_state = call(
        update_kernel,
        shape((mine, width, state_width), bf16),
        [driven, decay, state_input, state_held, scores],
        [VMEM] * 4 + [ANY],
        scratch=[
            pltpu.VMEM((mine, width, state_width), bf16),
            pltpu.SemaphoreType.DMA((mine, width // min(512, width))),
        ],
        limit=8,
        cost=4 * MIB,
        out_specs=ANY,
        name="state_update",
    )
    lines = 8 * mine
    shares, share, top = call(
        functools.partial(share_kernel, row_devices),
        [
            shape((lines, vocab * mine // lines + LANES), bf16),
            shape((mine, vocab)),
            shape((mine, LANES)),
        ],
        score_rows + [token_mask],
        [VMEM] * (row_devices + 1),
        scratch=[pltpu.VMEM((lines, vocab * mine // lines + LANES), f32)],
        name="share_of_peak",
    )
    every = lax.all_gather(shares, "head", axis=0)
    next_probs = call(
        probability_kernel,
        shape((mine, vocab), bf16),
        [every, share, top, floors],
        [VMEM] * 4,
        name="probabilities",
    )
    return (
        next_state.reshape(recurrent_state.shape),
        jnp.moveaxis(next_inner, 0, 1),
        jnp.moveaxis(next_group, 0, 1),
        layer_out,
        next_probs,
    )


def solution(mesh):
    in_specs = (
        P(None, "row"),
        P("row"),
        P("row", None, "head"),
        P("row", "head"),
        P("row", "head"),
        P(None, "head"),
        P(None, "head"),
        P("row", None, "head"),
        P("row", None, "head"),
        P("head"),
        P("head"),
        P("head"),
        P("row", "head", None, None),
        P("head"),
        P("head", "row"),
        P("row"),
        P("row", "head"),
        P("row", "head"),
        P("row"),
    )
    out_specs = (
        P("row", "head", None, None),
        P("row", None, "head"),
        P("row", None, "head"),
        P(None, "row"),
        P("row", "head"),
    )
    return jax.shard_map(local, mesh=mesh, in_specs=in_specs, out_specs=out_specs, check_vma=False)
```

```python
import functools

import jax
import jax.numpy as jnp
from jax import lax
from jax.experimental import pallas as pl
from jax.experimental.pallas import tpu as pltpu
from jax.sharding import PartitionSpec as P

D = 8192
HEADS = 256
HEAD_DIM = 64
GROUPS = 8
FIXED_BITS = 15.0

EPSILON = 1e-05
INVERSE_HEAT = 1.25
FIXED_POINT = 65536.0
NEG_LARGE = -1e30

MIB = 2**20
LANES = 128
TILE = 256
SHARES = (3, 12, 18, 24)
EARLY_INPUT = 6
VMEM = pl.BlockSpec(memory_space=pltpu.VMEM)
ANY = pl.BlockSpec(memory_space=pl.ANY)
f32 = jnp.float32
bf16 = jnp.bfloat16


def xor_permute(values, axis, distance):
    size = lax.axis_size(axis)
    return lax.ppermute(values, axis, [(at, at ^ distance) for at in range(size)])


def tree_sum(values):
    values = list(values)
    while len(values) > 1:
        values = [a + b for a, b in zip(values[0::2], values[1::2])]
    return values[0]


def split(values):
    high = values.astype(bf16)
    return high, (values - high.astype(f32)).astype(bf16)


def split_three(values):
    high, rest = split(values)
    middle = values - high.astype(f32)
    return high, rest, (middle - rest.astype(f32)).astype(bf16)


def silu(values):
    return values / (1.0 + jnp.exp(-values))


def dot(left, right):
    return jnp.dot(left, right, preferred_element_type=f32)


def dot_transposed(left, right):
    return lax.dot_general(left, right, (((1,), (1,)), ((), ())), preferred_element_type=f32)


def times_gain(values, gain_ref):
    return jnp.concatenate(
        [
            values[:, at * LANES : (at + 1) * LANES] * gain_ref[at : at + 1].astype(f32)
            for at in range(gain_ref.shape[0])
        ],
        axis=1,
    )


def beside_copies(body):
    pl.when(lax.axis_index("row") >= 0)(body)


def in_hbm(values):
    return pltpu.with_memory_space_constraint(values, pltpu.HBM)


def call(kernel, outs, operands, specs, scratch=(), limit=4, cost=0, out_specs=None, name=None):
    return pl.pallas_call(
        kernel,
        out_shape=outs,
        in_specs=specs,
        out_specs=out_specs if out_specs is not None else jax.tree.map(lambda _: VMEM, outs),
        scratch_shapes=list(scratch),
        compiler_params=pltpu.CompilerParams(vmem_limit_bytes=limit * MIB),
        cost_estimate=pl.CostEstimate(flops=1000, bytes_accessed=cost, transcendentals=0),
        name=name,
    )(*operands)


def shape(dims, dtype=f32):
    return jax.ShapeDtypeStruct(tuple(dims), dtype)


def group_kernel(keep, *refs):
    sources = refs[: keep + 3]
    weight_hbm, state_hbm, taps_hbm = sources[keep:]
    kept = refs[keep + 3 : 2 * keep + 3]
    part_ref, squares_ref, sent_ref, order, weight_ref, state_ref, taps_ref, stack, sems = refs[2 * keep + 3 :]
    places = list(kept) + [weight_ref, state_ref, taps_ref]
    copies = [
        pltpu.make_async_copy(source, place, sems.at[at])
        for at, (source, place) in enumerate(zip(sources, places))
    ]
    for copy in copies:
        copy.start()

    @beside_copies
    def _():
        regroup_matrix(order)
        stack[...] = jnp.zeros_like(stack)

    hidden_ref, gain_ref = kept[:2]
    rows = hidden_ref.shape[0]
    columns = weight_ref.shape[1]
    entries = columns // GROUPS
    devices = sent_ref.shape[0]
    for copy in copies:
        copy.wait()
    wide = hidden_ref[...].astype(f32)
    squares_ref[...] = jnp.broadcast_to(jnp.sum(wide * wide, axis=1, keepdims=True), squares_ref.shape)
    high, low = split(times_gain(wide, gain_ref))
    part = dot(jnp.concatenate([high, low], axis=0), weight_ref[...])
    part = part[:rows] + part[rows:]
    part_ref[...] = part
    part_high, part_low = split(part)
    stack[:rows] = part_high.astype(f32)
    stack[rows : 2 * rows] = part_low.astype(f32)
    for at in range(3):
        here = 2 * rows + at * state_ref.shape[1]
        stack[here : here + state_ref.shape[1]] = state_ref[at].astype(f32)
    tail = sent_ref.shape[1] - rows
    stack[2 * rows + tail : 2 * rows + tail + taps_ref.shape[0]] = taps_ref[...].astype(f32)
    grouped = dot(stack[...].astype(bf16), order[...])
    for device in range(devices):
        group = device // (devices // GROUPS)
        here = grouped[:, group * entries : (group + 1) * entries].astype(bf16)
        sent_ref[device, :rows, :entries] = here[:rows]
        sent_ref[device, :rows, entries:] = here[rows : 2 * rows]
        sent_ref[device, rows:, :entries] = here[2 * rows : 2 * rows + tail]
        sent_ref[device, rows:, entries:] = here[2 * rows + tail :]


def input_tile(weight_ref, at):
    depth, _, width = weight_ref.shape
    return weight_ref.reshape(2 * depth, width).at[:, pl.ds(at * LANES, LANES)]


def tile_moves(weight_ref, start, target, parts):
    size = target.shape[1] // parts
    return [
        (input_tile(weight_ref, start + tile).at[pl.ds(at * size, size)], target.at[tile, pl.ds(at * size, size)])
        for tile in range(target.shape[0])
        for at in range(parts)
    ]


def input_kernel(pieces, count, *refs):
    square_refs = refs[:pieces]
    hidden_ref, gain_ref, step_ref = refs[pieces : pieces + 3]
    tiles = list(refs[pieces + 3 : pieces + 3 + count])
    weight_ref, out_ref, small_ref, left, rest, sems = refs[pieces + 3 + count :]
    depth, _, width = weight_ref.shape
    rows = hidden_ref.shape[0]
    held = 2 * count
    parts = sems.shape[0] // rest.shape[0]
    copies = [
        pltpu.make_async_copy(source, place, sems.at[at])
        for at, (source, place) in enumerate(tile_moves(weight_ref, held, rest, parts))
    ]
    for copy in copies:
        copy.start()
    def project(first, pair):
        out_ref[:, first * LANES : (first + 2) * LANES] = dot(left[...], jnp.concatenate(pair, axis=1))

    @beside_copies
    def _():
        squares = tree_sum([ref[...] for ref in square_refs])[:, 0:1]
        scale = lax.rsqrt(squares / D + EPSILON)
        normed = times_gain(hidden_ref[...].astype(f32) * scale, gain_ref).astype(bf16).astype(f32)
        step = dot_transposed(normed.astype(bf16), step_ref[...])
        small_ref[...] = jnp.zeros_like(small_ref)
        small_ref[:, : step.shape[1]] = step
        small_ref[:, LANES:] = jnp.broadcast_to(scale, (rows, LANES))
        source = lax.broadcasted_iota(jnp.int32, (LANES, 4 * LANES), 0)
        target = lax.broadcasted_iota(jnp.int32, (LANES, 4 * LANES), 1)
        spread = 2 * source + target // (2 * LANES) == target % (2 * LANES)
        blocks = jnp.concatenate(
            [normed[:, block * LANES : (block + 1) * LANES] for block in range(depth // LANES)], axis=0
        )
        wide = dot(blocks.astype(bf16), spread.astype(f32).astype(bf16))
        for block in range(depth // LANES):
            here = wide[block * rows : (block + 1) * rows]
            left[:, 2 * block * LANES : 2 * (block + 1) * LANES] = jnp.concatenate(
                [here[:, : 2 * LANES], here[:, 2 * LANES :]], axis=0
            ).astype(bf16)
        for first in range(0, held, 2):
            project(first, [tiles[first // 2][0], tiles[first // 2][1]])

    for first in range(held, width // LANES, 2):
        for copy in copies[(first - held) * parts : (first - held + 2) * parts]:
            copy.wait()
        project(first, [rest[first - held], rest[first - held + 1]])


def pack_kernel(both_ref, part_ref, small_ref, arrived_ref, out_ref, held_ref):
    rows, width = small_ref.shape[0], both_ref.shape[1]
    blocks, mine, _ = out_ref.shape
    devices, _, double = arrived_ref.shape
    entries = double // 2
    columns = part_ref.shape[1]
    index = lax.axis_index("row")
    scale = small_ref[:, LANES : LANES + 1]
    arrived = arrived_ref[...].astype(f32)
    pair = (arrived[:, :rows, :entries] + arrived[:, :rows, entries:]) * scale[None]
    part = part_ref[...] * scale
    for device in range(devices):
        here = slice(device * entries, (device + 1) * entries)
        held_ref[0, :, here] = arrived[device, rows:, :entries]
        held_ref[1, :, here] = arrived[device, rows:, entries:]
    for block in range(blocks):
        place = block ^ index
        here = slice(block * mine, (block + 1) * mine)
        out_ref[place, :, :width] = both_ref[here]
        out_ref[place, :, width : 2 * width] = both_ref[rows + block * mine : rows + (block + 1) * mine]
        out_ref[place, :, 2 * width : 2 * width + columns] = part[here]
        out_ref[place, :, 2 * width + columns : 2 * width + columns + LANES] = small_ref[here, :LANES]
        start = 2 * width + columns + LANES
        for device in range(devices):
            out_ref[place, :, start + device * entries : start + (device + 1) * entries] = pair[device, here]


def state_kernel(finish, pieces, *refs):
    parts = [ref[...] for ref in refs[:pieces]]
    heads_ref, held_ref, inner_state_ref, inner_taps_ref = refs[pieces : pieces + 4]
    state_ref, gain_ref, spread_ref = refs[pieces + 4 : pieces + 7]
    mixer_ref, raw_ref, driven_ref, decay_ref, input_ref = refs[pieces + 7 :]
    total = tree_sum(parts)
    mine, width, state_width = state_ref.shape
    columns = raw_ref.shape[1] - width
    start = 2 * width + columns
    gate = total[:, :width]
    inner_raw = total[:, width : 2 * width].astype(bf16)
    raw_ref[...] = total[:, width:start]
    taps = inner_taps_ref[...].astype(f32)
    mixed = inner_raw.astype(f32) * taps[3:4]
    for at in range(3):
        mixed = mixed + inner_state_ref[at].astype(f32) * taps[at : at + 1]
    conv_inner = silu(mixed)
    taps = held_ref[1]
    mixed = total[:, start + LANES :].astype(bf16).astype(f32) * taps[3:4]
    for at in range(3):
        mixed = mixed + held_ref[0, at * mine : (at + 1) * mine] * taps[at : at + 1]
    pair = silu(mixed).astype(bf16)
    state_input = pair[:, :state_width].astype(f32)
    state_output = pair[:, state_width:]

    step_raw = total[:, start : start + LANES] + heads_ref[0:1]
    step_size = jnp.maximum(step_raw, 0.0) + jnp.log1p(jnp.exp(-jnp.abs(step_raw)))
    decay_rate = jnp.exp(-step_size * jnp.exp(heads_ref[1:2]))
    stacked = jnp.concatenate([step_size, decay_rate, heads_ref[2:3]], axis=0)
    parts = split_three(stacked)
    wide = (dot(parts[0], spread_ref[...]) + dot(parts[1], spread_ref[...])) + dot(parts[2], spread_ref[...])
    step_wide, decay_wide, skip_wide = wide[:mine], wide[mine : 2 * mine], wide[2 * mine :]
    driven = step_wide * conv_inner
    overlap = jnp.sum(state_input * state_output.astype(f32), axis=1, keepdims=True)
    old = jnp.concatenate(
        [dot_transposed(state_output, state_ref[row])[row : row + 1] for row in range(mine)], axis=0
    )
    readout = decay_wide * old + driven * overlap + skip_wide * conv_inner
    gated = readout * silu(gate)
    driven_ref[...] = driven
    decay_ref[...] = decay_wide
    input_ref[...] = state_input
    if finish:
        group_total = jnp.sum(gated * gated, axis=1, keepdims=True)
        group_scale = lax.rsqrt(group_total / (HEADS * HEAD_DIM // GROUPS) + EPSILON)
        gated = gated * group_scale * gain_ref[...].astype(f32)
    mixer_ref[...] = gated.astype(mixer_ref.dtype)


def update_kernel(
    driven_ref, decay_ref, input_ref, state_ref, raw_ref, inner_state_ref, group_state_ref, layer_ref, _, *refs
):
    out_ref, next_inner_ref, next_group_ref, layer_out_ref, new, sems = refs
    mine, width, _ = state_ref.shape
    block = min(512, width)
    blocks = width // block

    def copy(row, at):
        here = pl.ds(at * block, block)
        return pltpu.make_async_copy(new.at[row, here], out_ref.at[row, here], sems.at[row, at])

    for row in range(mine):
        both = jnp.concatenate(
            [driven_ref[row : row + 1], decay_ref[row : row + 1], jnp.zeros((6, width), f32)], axis=0
        )
        turned = jnp.transpose(both)
        for at in range(blocks):
            here = slice(at * block, (at + 1) * block)
            new[row, here] = (
                turned[here, 1:2] * state_ref[row, here].astype(f32)
                + turned[here, 0:1] * input_ref[row : row + 1]
            ).astype(bf16)
            copy(row, at).start()
    layer_out_ref[...] = layer_ref[...]
    next_inner_ref[0] = inner_state_ref[1]
    next_inner_ref[1] = inner_state_ref[2]
    next_inner_ref[2] = raw_ref[:, :width].astype(bf16)
    next_group_ref[0] = group_state_ref[1]
    next_group_ref[1] = group_state_ref[2]
    next_group_ref[2] = raw_ref[:, width:].astype(bf16)
    for row in range(mine):
        for at in range(blocks):
            copy(row, at).wait()


def output_kernel(pieces, *refs):
    weight_ref, _, out_ref, rows_held = refs[pieces:]
    index = lax.axis_index("row")
    for at in range(pieces):
        rows_held[index ^ at] = refs[at][...].astype(f32)
    left = jnp.concatenate([rows_held[at] for at in range(pieces)], axis=0).astype(bf16)
    width = weight_ref.shape[1]
    for column in range(0, width, TILE):
        out_ref[:, column : column + TILE] = dot(left, weight_ref[:, column : column + TILE])


def add_kernel(left_ref, right_ref, _, out_ref):
    out_ref[...] = left_ref[...] + right_ref[...]


def fixed_exponent(values):
    return jnp.floor(jnp.log2(jnp.maximum(values, 1e-30))) + 2.0


def lexicon_kernel(pieces, *refs):
    hidden_ref, gain_ref, mixed_ref = refs[:3]
    held_refs = refs[3 : 3 + pieces]
    weight_ref, layer_ref, out_ref, rest, left, scores, sems = refs[3 + pieces :]
    rows = hidden_ref.shape[0]
    blocks, mine, _ = out_ref.shape
    vocab = weight_ref.shape[1]
    done = vocab - rest.shape[1]
    part = rest.shape[1] // sems.shape[0]
    copies = [
        pltpu.make_async_copy(
            weight_ref.at[:, pl.ds(done + at * part, part)], rest.at[:, pl.ds(at * part, part)], sems.at[at]
        )
        for at in range(sems.shape[0])
    ]
    for copy in copies:
        copy.start()
    index = lax.axis_index("row")

    def put(value, column, width):
        value = value.astype(jnp.int32).astype(jnp.int16)
        for block in range(blocks):
            out_ref[block ^ index, :, column : column + width] = value[block * mine : (block + 1) * mine]

    def project(tile, column):
        term = dot(left[...], tile)
        scores[:, column : column + TILE] = term[:rows] + term[rows:]

    @beside_copies
    def _():
        layer = (hidden_ref[...].astype(f32) + mixed_ref[...]).astype(bf16)
        layer_ref[...] = layer
        wide = layer.astype(f32)
        squares = jnp.sum(wide * wide, axis=1, keepdims=True)
        high, low = split(wide * gain_ref[...].astype(f32))
        left[:rows] = high
        left[rows:] = low
        scores[:, vocab:] = jnp.broadcast_to(squares, (rows, LANES))
        base = 0
        for held in held_refs:
            for column in range(0, held.shape[1], TILE):
                project(held[:, column : column + TILE], base + column)
            base += held.shape[1]

    for column in range(0, rest.shape[1], TILE):
        if column % part == 0:
            copies[column // part].wait()
        project(rest[:, column : column + TILE], done + column)
    squares = scores[:, vocab : vocab + 1]
    peak = jnp.max(jnp.abs(scores[:, :vocab]), axis=1, keepdims=True)
    exponent = fixed_exponent(peak)
    square_exponent = fixed_exponent(squares)
    digits = squares * jnp.exp2(FIXED_BITS - square_exponent)
    digit = jnp.floor(digits)
    rest_digit = jnp.floor((digits - digit) * 2.0**FIXED_BITS)
    lane = lax.broadcasted_iota(jnp.int32, (rows, LANES), 1)
    tail = jnp.where(lane == 0, exponent, jnp.where(lane == 1, square_exponent, 0.0))
    put(jnp.where(lane == 2, digit, jnp.where(lane == 3, rest_digit, tail)), vocab, LANES)
    factor = jnp.exp2(FIXED_BITS - exponent)
    for column in range(0, vocab, 4 * TILE):
        put(jnp.round(scores[:, column : column + 4 * TILE] * factor), column, 4 * TILE)


def share_kernel(pieces, *refs):
    mask_ref, sent_ref, share_ref, top_ref, spread = refs[pieces:]
    mine, vocab = mask_ref.shape
    lines = sent_ref.shape[0] // mine
    part = vocab // lines
    terms, squares = [], []
    for ref in refs[:pieces]:
        tail = ref[:, vocab:].astype(jnp.int32).astype(f32)
        digits = tail[:, 2:3] + tail[:, 3:4] * 2.0**-FIXED_BITS
        squares.append(digits * jnp.exp2(tail[:, 1:2] - FIXED_BITS))
        terms.append(ref[:, :vocab].astype(jnp.int32).astype(f32) * jnp.exp2(tail[:, 0:1] - FIXED_BITS))
    scale = lax.rsqrt(tree_sum(squares) / D + EPSILON) * INVERSE_HEAT
    allowed = mask_ref[...] > 0
    logits = jnp.where(allowed, tree_sum(terms) * scale, NEG_LARGE)
    top = jnp.max(logits, axis=1, keepdims=True)
    share = jnp.where(allowed, jnp.exp(logits - top), 0.0)
    share_ref[...] = share
    top_ref[...] = jnp.broadcast_to(top, top_ref.shape)
    spread[...] = jnp.zeros_like(spread)
    parts = [value.astype(f32) for value in split_three(top)]
    for row in range(mine):
        for line in range(lines):
            here = slice(row * lines + line, row * lines + line + 1)
            spread[here, :part] = share[row : row + 1, line * part : (line + 1) * part]
        here = slice(row * lines, (row + 1) * lines)
        for at in range(3):
            spread[here, part + at : part + at + 1] = jnp.broadcast_to(parts[at][row : row + 1], (lines, 1))
    sent_ref[...] = spread[...].astype(bf16)


def weigh(relative, inverse_floor):
    return relative * jnp.clip(relative * inverse_floor - 1.0, 0.0, 1.0)


def probability_kernel(every_ref, share_ref, top_ref, floor_ref, out_ref):
    mine, vocab = share_ref.shape
    devices, lines, _ = every_ref.shape
    part = vocab * mine // lines
    inverse = FIXED_POINT / floor_ref[:, 0:1].astype(f32)
    tops = [
        jnp.sum(every_ref[device, :, part:].astype(f32), axis=1, keepdims=True)
        for device in range(devices)
    ]
    peak = functools.reduce(jnp.maximum, tops)
    per_row = lines // mine
    spread = jnp.concatenate(
        [jnp.broadcast_to(inverse[row : row + 1], (per_row, 1)) for row in range(mine)], axis=0
    )
    kept = jnp.zeros((lines, part), f32)
    for device in range(devices):
        relative = every_ref[device, :, :part].astype(f32) * jnp.exp(tops[device] - peak)
        kept = kept + weigh(relative, spread)
    kept = jnp.sum(kept, axis=1, keepdims=True)
    total = jnp.concatenate(
        [jnp.sum(kept[row * per_row : (row + 1) * per_row], axis=0, keepdims=True) for row in range(mine)],
        axis=0,
    )
    highest = jnp.concatenate([peak[row * per_row : row * per_row + 1] for row in range(mine)], axis=0)
    own = weigh(share_ref[...] * jnp.exp(top_ref[:, 0:1] - highest), inverse)
    out_ref[...] = (own / total).astype(bf16)


def regroup_matrix(ref):
    columns = ref.shape[0]
    source = lax.broadcasted_iota(jnp.int32, ref.shape, 0)
    target = lax.broadcasted_iota(jnp.int32, ref.shape, 1)
    order = (source % GROUPS) * (columns // GROUPS) + source // GROUPS == target
    ref[...] = order.astype(f32).astype(bf16)


def head_matrix(ref):
    head = lax.broadcasted_iota(jnp.int32, ref.shape, 0)
    channel = lax.broadcasted_iota(jnp.int32, ref.shape, 1)
    ref[...] = (channel // HEAD_DIM == head).astype(f32).astype(bf16)


def fetch_kernel(count, jobs, makes, *refs):
    sources = refs[:count]
    targets = refs[count + 1 : count + 1 + len(jobs)]
    made = refs[count + 1 + len(jobs) : -1]
    sems = refs[-1]
    copies = []
    for (at, kind, start), target in zip(jobs, targets):
        if kind == "whole":
            moves = [(sources[at], target)]
        elif kind == "columns":
            moves = [(sources[at].at[:, pl.ds(start, target.shape[1])], target)]
        else:
            moves = tile_moves(sources[at], start, target, 1)
        for source, place in moves:
            copies.append(pltpu.make_async_copy(source, place, sems.at[len(copies)]))
    for copy in copies:
        copy.start()
    if makes:

        @beside_copies
        def _():
            for make, ref in zip(makes, made):
                make(ref)

    for copy in copies:
        copy.wait()


def fetch(jobs, after, name, makes=()):
    jobs = [job for job in jobs if 0 not in job[3]]
    if not jobs and not makes:
        return []
    sources = []
    for source, *_ in jobs:
        if not any(source is other for other in sources):
            sources.append(source)
    plan = [
        ([source is other for other in sources].index(True), kind, start) for source, kind, start, _ in jobs
    ]
    outs = [pltpu.VMEM(dims, bf16) for *_, dims in jobs] + [pltpu.VMEM(dims, bf16) for _, dims in makes]
    size = sum(2 * functools.reduce(lambda a, b: a * b, dims) for *_, dims in jobs)
    return list(call(
        functools.partial(fetch_kernel, len(sources), plan, [make for make, _ in makes]),
        outs,
        [in_hbm(source) for source in sources] + [after],
        [ANY] * (len(sources) + 1),
        scratch=[pltpu.SemaphoreType.DMA((sum(dims[0] if kind == "tiles" else 1 for _, kind, _, dims in jobs),))],
        limit=2,
        cost=size,
        out_specs=[VMEM] * len(outs),
        name=name,
    ))


def local(
    hidden,
    norm_gain,
    input_weight,
    group_weight,
    step_weight,
    conv_inner_weight,
    conv_group_weight,
    conv_inner_state,
    conv_group_state,
    timestep_bias,
    decay_log,
    skip_gain,
    recurrent_state,
    mixer_gain,
    output_weight,
    final_gain,
    lexicon_matrix,
    token_mask,
    min_share,
):
    mine, heads_mine, head_width, state_width = recurrent_state.shape
    width = heads_mine * head_width
    rows, depth = hidden.shape
    vocab = lexicon_matrix.shape[1]
    row_devices = lax.axis_size("row")
    head_devices = lax.axis_size("head")
    group_devices = head_devices // GROUPS
    columns = group_weight.shape[1]
    entries = columns // GROUPS
    held_rows = -(-3 * mine // 8) * 8

    heads = jnp.pad(
        jnp.stack([timestep_bias, decay_log, skip_gain]), ((0, 0), (0, LANES - heads_mine))
    )
    inner_state = jnp.moveaxis(conv_inner_state, 1, 0)
    group_state = jnp.moveaxis(conv_group_state, 1, 0)
    state = recurrent_state.reshape(mine, width, state_width)
    floors = jnp.broadcast_to(min_share[:, None], (mine, LANES))

    kept_arrays = [hidden, norm_gain.reshape(-1, LANES), step_weight.T]
    used_arrays = [group_weight, group_state, conv_group_weight]
    hidden_held, gain_held, step_held, group_part, squares, sent = call(
        functools.partial(group_kernel, len(kept_arrays)),
        [pltpu.VMEM(array.shape, array.dtype) for array in kept_arrays]
        + [
            shape((rows, columns)),
            shape((rows, LANES)),
            shape((head_devices, rows + held_rows, 2 * entries), bf16),
        ],
        [in_hbm(array) for array in kept_arrays + used_arrays],
        [ANY] * 6,
        scratch=[pltpu.VMEM((columns, columns), bf16)]
        + [pltpu.VMEM(array.shape, array.dtype) for array in used_arrays]
        + [
            pltpu.VMEM((2 * rows + 2 * held_rows, columns), f32),
            pltpu.SemaphoreType.DMA((6,)),
        ],
        limit=6,
        cost=2 * MIB,
        out_specs=[VMEM] * 6,
        name="group_projection",
    )
    arrived = lax.all_to_all(sent, "head", 0, 0, tiled=True)
    all_squares = [squares] + [xor_permute(squares, "row", at) for at in range(1, row_devices)]
    pairs = width // TILE
    early = 2 * (pairs * EARLY_INPUT // 8)
    late = width // LANES - early
    input_held = fetch(
        [(input_weight, "tiles", at, (2, 2 * depth, LANES)) for at in range(0, early, 2)],
        arrived,
        "fetch_input",
    )
    parts = 1
    both, small = call(
        functools.partial(input_kernel, row_devices, len(input_held)),
        [shape((2 * rows, width)), shape((rows, 2 * LANES))],
        all_squares + [hidden_held, gain_held, step_held] + input_held + [in_hbm(input_weight)],
        [VMEM] * (row_devices + 3 + len(input_held)) + [ANY],
        scratch=[
            pltpu.VMEM((2 * rows, 2 * depth), bf16),
            pltpu.VMEM((late, 2 * depth, LANES), bf16),
            pltpu.SemaphoreType.DMA((late * parts,)),
        ],
        limit=late + 6,
        cost=2 * input_weight.size,
        name="input_projection",
    )
    tiles = vocab // TILE
    cuts = [tiles * share // 32 * TILE for share in SHARES]
    spans = [(start, end - start) for start, end in zip([0] + cuts[:-1], cuts)]
    fetched = []

    def lexicon_job(stage):
        start, size = spans[stage]
        return (lexicon_matrix, "columns", start, (depth, size))

    def fetch_lexicon(stage, after, name):
        if not spans[stage][1]:
            return after
        fetched.extend(fetch([lexicon_job(stage)], after, name))
        return fetched[-1]

    packed_width = 2 * width + columns + LANES + 2 * state_width
    packed, held = call(
        pack_kernel,
        [shape((row_devices, mine, packed_width)), shape((2, held_rows, 2 * state_width))],
        [both, group_part, small, arrived],
        [VMEM] * 4,
        name="pack_rows",
    )
    pieces = [packed[0]] + [xor_permute(packed[at], "row", at) for at in range(1, row_devices)]

    output_held, state_held, *fetched, spread = fetch(
        [
            (output_weight, "whole", 0, output_weight.shape),
            (state, "whole", 0, state.shape),
            lexicon_job(0),
        ],
        packed,
        "fetch_output",
        [(head_matrix, (LANES, width))],
    )
    finish = group_devices == 1
    mixer_in, raw, driven, decay, state_input = call(
        functools.partial(state_kernel, finish, row_devices),
        [
            shape((mine, width), bf16 if finish else f32),
            shape((mine, width + columns)),
            shape((mine, width)),
            shape((mine, width)),
            shape((mine, state_width)),
        ],
        pieces + [heads, held, inner_state, conv_inner_weight, state_held, mixer_gain[None], spread],
        [VMEM] * (row_devices + 7),
        limit=8,
        cost=2 * MIB,
        name="state_readout",
    )
    if not finish:
        members = [
            [group * group_devices + at for at in range(group_devices)] for group in range(GROUPS)
        ]
        group_total = lax.psum(jnp.sum(mixer_in * mixer_in, axis=1), "head", axis_index_groups=members)
        group_scale = lax.rsqrt(group_total / (HEADS * HEAD_DIM // GROUPS) + EPSILON)
        mixer_in = (mixer_in * group_scale[:, None] * mixer_gain.astype(f32)[None]).astype(bf16)

    mixer_rows = [mixer_in] + [xor_permute(mixer_in, "row", at) for at in range(1, row_devices)]
    ahead = fetch_lexicon(1, mixer_in, "fetch_lexicon_1")
    mixed = call(
        functools.partial(output_kernel, row_devices),
        shape((rows, depth)),
        mixer_rows + [output_held, ahead],
        [VMEM] * (row_devices + 1) + [ANY],
        scratch=[pltpu.VMEM((row_devices, mine, width), f32)],
        cost=4 * MIB,
        name="output_projection",
    )
    distance = 1
    while distance < head_devices:
        other = xor_permute(mixed, "head", distance)
        ahead = mixed
        for stage, place in ((2, head_devices // 4), (3, head_devices // 2)):
            if distance == place:
                ahead = fetch_lexicon(stage, mixed, f"fetch_lexicon_{stage}")
        mixed = call(
            add_kernel, shape((rows, depth)), [mixed, other, ahead], [VMEM, VMEM, ANY], name="add"
        )
        distance *= 2
    layer, scores = call(
        functools.partial(lexicon_kernel, len(fetched)),
        [pltpu.VMEM((rows, depth), bf16), shape((row_devices, mine, vocab + LANES), jnp.int16)],
        [hidden_held, final_gain[None], mixed] + fetched + [in_hbm(lexicon_matrix)],
        [VMEM] * (3 + len(fetched)) + [ANY],
        scratch=[
            pltpu.VMEM((depth, vocab - cuts[-1]), bf16),
            pltpu.VMEM((2 * rows, depth), bf16),
            pltpu.VMEM((rows, vocab + LANES), f32),
            pltpu.SemaphoreType.DMA((max(1, (vocab - cuts[-1]) // (2 * TILE)),)),
        ],
        limit=16,
        cost=16 * MIB,
        name="lexicon_projection",
    )
    score_rows = [scores[0]] + [xor_permute(scores[at], "row", at) for at in range(1, row_devices)]
    next_state, next_inner, next_group, layer_out = call(
        update_kernel,
        [
            shape((mine, width, state_width), bf16),
            shape((3, mine, width), bf16),
            shape((3, mine, columns), bf16),
            shape((rows, depth), bf16),
        ],
        [driven, decay, state_input, state_held, raw, inner_state, group_state, layer, scores],
        [VMEM] * 8 + [ANY],
        scratch=[
            pltpu.VMEM((mine, width, state_width), bf16),
            pltpu.SemaphoreType.DMA((mine, width // min(512, width))),
        ],
        limit=8,
        cost=4 * MIB,
        out_specs=[ANY, VMEM, VMEM, VMEM],
        name="state_update",
    )
    lines = 8 * mine
    shares, share, top = call(
        functools.partial(share_kernel, row_devices),
        [
            shape((lines, vocab * mine // lines + LANES), bf16),
            shape((mine, vocab)),
            shape((mine, LANES)),
        ],
        score_rows + [token_mask],
        [VMEM] * (row_devices + 1),
        scratch=[pltpu.VMEM((lines, vocab * mine // lines + LANES), f32)],
        name="share_of_peak",
    )
    every = lax.all_gather(shares, "head", axis=0)
    next_probs = call(
        probability_kernel,
        shape((mine, vocab), bf16),
        [every, share, top, floors],
        [VMEM] * 4,
        name="probabilities",
    )
    return (
        next_state.reshape(recurrent_state.shape),
        jnp.moveaxis(next_inner, 0, 1),
        jnp.moveaxis(next_group, 0, 1),
        layer_out,
        next_probs,
    )


def solution(mesh):
    in_specs = (
        P(None, "row"),
        P("row"),
        P("row", None, "head"),
        P("row", "head"),
        P("row", "head"),
        P(None, "head"),
        P(None, "head"),
        P("row", None, "head"),
        P("row", None, "head"),
        P("head"),
        P("head"),
        P("head"),
        P("row", "head", None, None),
        P("head"),
        P("head", "row"),
        P("row"),
        P("row", "head"),
        P("row", "head"),
        P("row"),
    )
    out_specs = (
        P("row", "head", None, None),
        P("row", None, "head"),
        P("row", None, "head"),
        P(None, "row"),
        P("row", "head"),
    )
    return jax.shard_map(local, mesh=mesh, in_specs=in_specs, out_specs=out_specs, check_vma=False)
```

```python
import functools

import jax
import jax.numpy as jnp
from jax import lax
from jax.experimental import pallas as pl
from jax.experimental.pallas import tpu as pltpu
from jax.sharding import PartitionSpec as P

D = 8192
HEADS = 256
HEAD_DIM = 64
GROUPS = 8
FIXED_BITS = 15.0

EPSILON = 1e-05
INVERSE_HEAT = 1.25
FIXED_POINT = 65536.0
NEG_LARGE = -1e30

MIB = 2**20
LANES = 128
TILE = 256
SHARES = (7, 15, 26)
EARLY_INPUT = 6
VMEM = pl.BlockSpec(memory_space=pltpu.VMEM)
ANY = pl.BlockSpec(memory_space=pl.ANY)
f32 = jnp.float32
bf16 = jnp.bfloat16


def xor_permute(values, axis, distance):
    size = lax.axis_size(axis)
    return lax.ppermute(values, axis, [(at, at ^ distance) for at in range(size)])


def row_send(values, distance):
    size = lax.axis_size("row")
    return lax.ppermute(values, "row", [(at, (at + distance) % size) for at in range(size)])


def row_place(block, index, count):
    return lax.rem(block - index + count, count)


def row_origin(index, distance, count):
    return lax.rem(index - distance + count, count)


def tree_sum(values):
    values = list(values)
    while len(values) > 1:
        values = [a + b for a, b in zip(values[0::2], values[1::2])]
    return values[0]


def split(values):
    high = values.astype(bf16)
    return high, (values - high.astype(f32)).astype(bf16)


def split_three(values):
    high, rest = split(values)
    middle = values - high.astype(f32)
    return high, rest, (middle - rest.astype(f32)).astype(bf16)


def silu(values):
    return values / (1.0 + jnp.exp(-values))


def dot(left, right):
    return jnp.dot(left, right, preferred_element_type=f32)


def dot_transposed(left, right):
    return lax.dot_general(left, right, (((1,), (1,)), ((), ())), preferred_element_type=f32)


def times_gain(values, gain_ref):
    return jnp.concatenate(
        [
            values[:, at * LANES : (at + 1) * LANES] * gain_ref[at : at + 1].astype(f32)
            for at in range(gain_ref.shape[0])
        ],
        axis=1,
    )


def beside_copies(body):
    pl.when(lax.axis_index("row") >= 0)(body)


def in_hbm(values):
    return pltpu.with_memory_space_constraint(values, pltpu.HBM)


def call(kernel, outs, operands, specs, scratch=(), limit=4, cost=0, out_specs=None, name=None):
    return pl.pallas_call(
        kernel,
        out_shape=outs,
        in_specs=specs,
        out_specs=out_specs if out_specs is not None else jax.tree.map(lambda _: VMEM, outs),
        scratch_shapes=list(scratch),
        compiler_params=pltpu.CompilerParams(vmem_limit_bytes=limit * MIB),
        cost_estimate=pl.CostEstimate(flops=1000, bytes_accessed=cost, transcendentals=0),
        name=name,
    )(*operands)


def shape(dims, dtype=f32):
    return jax.ShapeDtypeStruct(tuple(dims), dtype)


def group_kernel(keep, *refs):
    sources = refs[: keep + 3]
    weight_hbm, state_hbm, taps_hbm = sources[keep:]
    kept = refs[keep + 3 : 2 * keep + 3]
    part_ref, squares_ref, sent_ref, order, weight_ref, state_ref, taps_ref, stack, sems = refs[2 * keep + 3 :]
    places = list(kept) + [weight_ref, state_ref, taps_ref]
    copies = [
        pltpu.make_async_copy(source, place, sems.at[at])
        for at, (source, place) in enumerate(zip(sources, places))
    ]
    for copy in copies:
        copy.start()

    @beside_copies
    def _():
        regroup_matrix(order)
        stack[...] = jnp.zeros_like(stack)

    hidden_ref, gain_ref = kept[:2]
    rows = hidden_ref.shape[0]
    columns = weight_ref.shape[1]
    entries = columns // GROUPS
    devices = sent_ref.shape[0]
    for copy in copies:
        copy.wait()
    wide = hidden_ref[...].astype(f32)
    squares_ref[...] = jnp.broadcast_to(jnp.sum(wide * wide, axis=1, keepdims=True), squares_ref.shape)
    high, low = split(times_gain(wide, gain_ref))
    part = dot(jnp.concatenate([high, low], axis=0), weight_ref[...])
    part = part[:rows] + part[rows:]
    part_ref[...] = part
    part_high, part_low = split(part)
    stack[:rows] = part_high.astype(f32)
    stack[rows : 2 * rows] = part_low.astype(f32)
    taps = taps_ref[...].astype(f32)
    for side in range(2):
        here = 2 * rows + 8 * side
        for at in range(3):
            stack[here + at : here + at + 1] = state_ref[at, side : side + 1].astype(f32)
        for at in range(2):
            stack[here + 3 + at : here + 4 + at] = taps[2 * at + side : 2 * at + side + 1]
    grouped = dot(stack[...].astype(bf16), order[...])
    each = devices // GROUPS
    for group in range(GROUPS):
        here = grouped[:, group * entries : (group + 1) * entries]
        first = jnp.concatenate([here[:rows], here[2 * rows : 2 * rows + 8]], axis=0)
        second = jnp.concatenate([here[rows : 2 * rows], here[2 * rows + 8 :]], axis=0)
        value = jnp.concatenate([first, second], axis=1).astype(bf16)
        for at in range(each):
            sent_ref[group * each + at] = value


def input_tile(weight_ref, at):
    depth, _, width = weight_ref.shape
    return weight_ref.reshape(2 * depth, width).at[:, pl.ds(at * LANES, LANES)]


def tile_moves(weight_ref, start, target, parts):
    size = target.shape[1] // parts
    return [
        (input_tile(weight_ref, start + tile).at[pl.ds(at * size, size)], target.at[tile, pl.ds(at * size, size)])
        for tile in range(target.shape[0])
        for at in range(parts)
    ]


def input_kernel(pieces, count, *refs):
    square_refs = refs[:pieces]
    hidden_ref, gain_ref, step_ref = refs[pieces : pieces + 3]
    tiles = list(refs[pieces + 3 : pieces + 3 + count])
    weight_ref, out_ref, small_ref, left, rest, sems = refs[pieces + 3 + count :]
    depth, _, width = weight_ref.shape
    rows = hidden_ref.shape[0]
    held = 2 * count
    parts = sems.shape[0] // rest.shape[0]
    copies = [
        pltpu.make_async_copy(source, place, sems.at[at])
        for at, (source, place) in enumerate(tile_moves(weight_ref, held, rest, parts))
    ]
    for copy in copies:
        copy.start()
    def project(first, pair):
        out_ref[:, first * LANES : (first + 2) * LANES] = dot(left[...], jnp.concatenate(pair, axis=1))

    @beside_copies
    def _():
        squares = tree_sum([ref[...] for ref in square_refs])[:, 0:1]
        scale = lax.rsqrt(squares / D + EPSILON)
        normed = times_gain(hidden_ref[...].astype(f32) * scale, gain_ref).astype(bf16).astype(f32)
        step = dot_transposed(normed.astype(bf16), step_ref[...])
        small_ref[...] = jnp.zeros_like(small_ref)
        small_ref[:, : step.shape[1]] = step
        small_ref[:, LANES:] = jnp.broadcast_to(scale, (rows, LANES))
        source = lax.broadcasted_iota(jnp.int32, (LANES, 4 * LANES), 0)
        target = lax.broadcasted_iota(jnp.int32, (LANES, 4 * LANES), 1)
        spread = 2 * source + target // (2 * LANES) == target % (2 * LANES)
        blocks = jnp.concatenate(
            [normed[:, block * LANES : (block + 1) * LANES] for block in range(depth // LANES)], axis=0
        )
        wide = dot(blocks.astype(bf16), spread.astype(f32).astype(bf16))
        for block in range(depth // LANES):
            here = wide[block * rows : (block + 1) * rows]
            left[:, 2 * block * LANES : 2 * (block + 1) * LANES] = jnp.concatenate(
                [here[:, : 2 * LANES], here[:, 2 * LANES :]], axis=0
            ).astype(bf16)
        for first in range(0, held, 2):
            project(first, [tiles[first // 2][0], tiles[first // 2][1]])

    for first in range(held, width // LANES, 2):
        for copy in copies[(first - held) * parts : (first - held + 2) * parts]:
            copy.wait()
        project(first, [rest[first - held], rest[first - held + 1]])


def pack_kernel(both_ref, part_ref, small_ref, arrived_ref, out_ref, held_ref):
    rows, width = small_ref.shape[0], both_ref.shape[1]
    blocks, mine, _ = out_ref.shape
    devices, _, double = arrived_ref.shape
    entries = double // 2
    columns = part_ref.shape[1]
    index = lax.axis_index("row")
    scale = small_ref[:, LANES : LANES + 1]
    arrived = arrived_ref[...].astype(f32)
    pair = (arrived[:, :rows, :entries] + arrived[:, :rows, entries:]) * scale[None]
    part = part_ref[...] * scale
    held_ref[...] = jnp.zeros_like(held_ref)
    for device in range(devices):
        here = slice(device * entries, (device + 1) * entries)
        for side in range(2):
            lines = arrived[device, rows:, side * entries : (side + 1) * entries]
            for at in range(3):
                held_ref[0, at * mine + side : at * mine + side + 1, here] = lines[at : at + 1]
            for at in range(2):
                held_ref[1, 2 * at + side : 2 * at + side + 1, here] = lines[3 + at : 4 + at]
    for block in range(blocks):
        place = row_place(block, index, blocks)
        here = slice(block * mine, (block + 1) * mine)
        out_ref[place, :, :width] = both_ref[here]
        out_ref[place, :, width : 2 * width] = both_ref[rows + block * mine : rows + (block + 1) * mine]
        out_ref[place, :, 2 * width : 2 * width + columns] = part[here]
        out_ref[place, :, 2 * width + columns : 2 * width + columns + LANES] = small_ref[here, :LANES]
        start = 2 * width + columns + LANES
        for device in range(devices):
            out_ref[place, :, start + device * entries : start + (device + 1) * entries] = pair[device, here]


def state_kernel(finish, pieces, *refs):
    parts = [ref[...] for ref in refs[:pieces]]
    heads_ref, held_ref, inner_state_ref, inner_taps_ref = refs[pieces : pieces + 4]
    state_ref, gain_ref, spread_ref = refs[pieces + 4 : pieces + 7]
    mixer_ref, raw_ref, driven_ref, decay_ref, input_ref = refs[pieces + 7 :]
    total = tree_sum(parts)
    mine, width, state_width = state_ref.shape
    columns = raw_ref.shape[1] - width
    start = 2 * width + columns
    gate = total[:, :width]
    inner_raw = total[:, width : 2 * width].astype(bf16)
    raw_ref[...] = total[:, width:start]
    taps = inner_taps_ref[...].astype(f32)
    mixed = inner_raw.astype(f32) * taps[3:4]
    for at in range(3):
        mixed = mixed + inner_state_ref[at].astype(f32) * taps[at : at + 1]
    conv_inner = silu(mixed)
    taps = held_ref[1]
    mixed = total[:, start + LANES :].astype(bf16).astype(f32) * taps[3:4]
    for at in range(3):
        mixed = mixed + held_ref[0, at * mine : (at + 1) * mine] * taps[at : at + 1]
    pair = silu(mixed).astype(bf16)
    state_input = pair[:, :state_width].astype(f32)
    state_output = pair[:, state_width:]

    step_raw = total[:, start : start + LANES] + heads_ref[0:1]
    step_size = jnp.maximum(step_raw, 0.0) + jnp.log1p(jnp.exp(-jnp.abs(step_raw)))
    decay_rate = jnp.exp(-step_size * jnp.exp(heads_ref[1:2]))
    stacked = jnp.concatenate([step_size, decay_rate, heads_ref[2:3]], axis=0)
    parts = split_three(stacked)
    wide = (dot(parts[0], spread_ref[...]) + dot(parts[1], spread_ref[...])) + dot(parts[2], spread_ref[...])
    step_wide, decay_wide, skip_wide = wide[:mine], wide[mine : 2 * mine], wide[2 * mine :]
    driven = step_wide * conv_inner
    overlap = jnp.sum(state_input * state_output.astype(f32), axis=1, keepdims=True)
    old = jnp.concatenate(
        [dot_transposed(state_output, state_ref[row])[row : row + 1] for row in range(mine)], axis=0
    )
    readout = decay_wide * old + driven * overlap + skip_wide * conv_inner
    gated = readout * silu(gate)
    driven_ref[...] = driven
    decay_ref[...] = decay_wide
    input_ref[...] = state_input
    if finish:
        group_total = jnp.sum(gated * gated, axis=1, keepdims=True)
        group_scale = lax.rsqrt(group_total / (HEADS * HEAD_DIM // GROUPS) + EPSILON)
        gated = gated * group_scale * gain_ref[...].astype(f32)
    mixer_ref[...] = gated.astype(mixer_ref.dtype)


def update_kernel(
    driven_ref, decay_ref, input_ref, state_ref, raw_ref, inner_state_ref, group_state_ref, layer_ref, _, *refs
):
    out_ref, next_inner_ref, next_group_ref, layer_out_ref, new, sems = refs
    mine, width, _ = state_ref.shape
    block = min(512, width)
    blocks = width // block

    def copy(row, at):
        here = pl.ds(at * block, block)
        return pltpu.make_async_copy(new.at[row, here], out_ref.at[row, here], sems.at[row, at])

    for row in range(mine):
        both = jnp.concatenate(
            [driven_ref[row : row + 1], decay_ref[row : row + 1], jnp.zeros((6, width), f32)], axis=0
        )
        turned = jnp.transpose(both)
        for at in range(blocks):
            here = slice(at * block, (at + 1) * block)
            new[row, here] = (
                turned[here, 1:2] * state_ref[row, here].astype(f32)
                + turned[here, 0:1] * input_ref[row : row + 1]
            ).astype(bf16)
            copy(row, at).start()
    layer_out_ref[...] = layer_ref[...]
    next_inner_ref[0] = inner_state_ref[1]
    next_inner_ref[1] = inner_state_ref[2]
    next_inner_ref[2] = raw_ref[:, :width].astype(bf16)
    next_group_ref[0] = group_state_ref[1]
    next_group_ref[1] = group_state_ref[2]
    next_group_ref[2] = raw_ref[:, width:].astype(bf16)
    for row in range(mine):
        for at in range(blocks):
            copy(row, at).wait()


def output_kernel(pieces, *refs):
    weight_ref, _, out_ref, rows_held = refs[pieces:]
    index = lax.axis_index("row")
    for at in range(pieces):
        rows_held[row_origin(index, at, pieces)] = refs[at][...].astype(f32)
    left = jnp.concatenate([rows_held[at] for at in range(pieces)], axis=0).astype(bf16)
    width = weight_ref.shape[1]
    for column in range(0, width, TILE):
        out_ref[:, column : column + TILE] = dot(left, weight_ref[:, column : column + TILE])


def add_kernel(count, *refs):
    refs[-1][...] = tree_sum([ref[...] for ref in refs[:count]])


def fixed_exponent(values):
    return jnp.floor(jnp.log2(jnp.maximum(values, 1e-30))) + 2.0


def lexicon_kernel(pieces, *refs):
    hidden_ref, gain_ref, mixed_ref = refs[:3]
    held_refs = refs[3 : 3 + pieces]
    weight_ref, layer_ref, out_ref, rest, left, scores, sems = refs[3 + pieces :]
    rows = hidden_ref.shape[0]
    blocks, mine, _ = out_ref.shape
    vocab = weight_ref.shape[1]
    done = vocab - rest.shape[1]
    part = rest.shape[1] // sems.shape[0]
    copies = [
        pltpu.make_async_copy(
            weight_ref.at[:, pl.ds(done + at * part, part)], rest.at[:, pl.ds(at * part, part)], sems.at[at]
        )
        for at in range(sems.shape[0])
    ]
    for copy in copies:
        copy.start()
    index = lax.axis_index("row")

    def put(value, column, width):
        value = value.astype(jnp.int32).astype(jnp.int16)
        for block in range(blocks):
            out_ref[row_place(block, index, blocks), :, column : column + width] = value[block * mine : (block + 1) * mine]

    def project(tile, column):
        term = dot(left[...], tile)
        scores[:, column : column + TILE] = term[:rows] + term[rows:]

    @beside_copies
    def _():
        layer = (hidden_ref[...].astype(f32) + mixed_ref[...]).astype(bf16)
        layer_ref[...] = layer
        wide = layer.astype(f32)
        squares = jnp.sum(wide * wide, axis=1, keepdims=True)
        high, low = split(wide * gain_ref[...].astype(f32))
        left[:rows] = high
        left[rows:] = low
        scores[:, vocab:] = jnp.broadcast_to(squares, (rows, LANES))
        base = 0
        for held in held_refs:
            for column in range(0, held.shape[1], TILE):
                project(held[:, column : column + TILE], base + column)
            base += held.shape[1]

    for column in range(0, rest.shape[1], TILE):
        if column % part == 0:
            copies[column // part].wait()
        project(rest[:, column : column + TILE], done + column)
    squares = scores[:, vocab : vocab + 1]
    peak = jnp.max(jnp.abs(scores[:, :vocab]), axis=1, keepdims=True)
    exponent = fixed_exponent(peak)
    square_exponent = fixed_exponent(squares)
    digits = squares * jnp.exp2(FIXED_BITS - square_exponent)
    digit = jnp.floor(digits)
    rest_digit = jnp.floor((digits - digit) * 2.0**FIXED_BITS)
    lane = lax.broadcasted_iota(jnp.int32, (rows, LANES), 1)
    tail = jnp.where(lane == 0, exponent, jnp.where(lane == 1, square_exponent, 0.0))
    put(jnp.where(lane == 2, digit, jnp.where(lane == 3, rest_digit, tail)), vocab, LANES)
    factor = jnp.exp2(FIXED_BITS - exponent)
    for column in range(0, vocab, 4 * TILE):
        put(jnp.round(scores[:, column : column + 4 * TILE] * factor), column, 4 * TILE)


def share_kernel(pieces, *refs):
    mask_ref, sent_ref, share_ref, top_ref, spread = refs[pieces:]
    mine, vocab = mask_ref.shape
    lines = sent_ref.shape[0] // mine
    part = vocab // lines
    terms, squares = [], []
    for ref in refs[:pieces]:
        tail = ref[:, vocab:].astype(jnp.int32).astype(f32)
        digits = tail[:, 2:3] + tail[:, 3:4] * 2.0**-FIXED_BITS
        squares.append(digits * jnp.exp2(tail[:, 1:2] - FIXED_BITS))
        terms.append(ref[:, :vocab].astype(jnp.int32).astype(f32) * jnp.exp2(tail[:, 0:1] - FIXED_BITS))
    scale = lax.rsqrt(tree_sum(squares) / D + EPSILON) * INVERSE_HEAT
    allowed = mask_ref[...] > 0
    logits = jnp.where(allowed, tree_sum(terms) * scale, NEG_LARGE)
    top = jnp.max(logits, axis=1, keepdims=True)
    share = jnp.where(allowed, jnp.exp(logits - top), 0.0)
    share_ref[...] = share
    top_ref[...] = jnp.broadcast_to(top, top_ref.shape)
    spread[...] = jnp.zeros_like(spread)
    parts = [value.astype(f32) for value in split_three(top)]
    for row in range(mine):
        for line in range(lines):
            here = slice(row * lines + line, row * lines + line + 1)
            spread[here, :part] = share[row : row + 1, line * part : (line + 1) * part]
        here = slice(row * lines, (row + 1) * lines)
        for at in range(3):
            spread[here, part + at : part + at + 1] = jnp.broadcast_to(parts[at][row : row + 1], (lines, 1))
    sent_ref[...] = spread[...].astype(bf16)


def weigh(relative, inverse_floor):
    return relative * jnp.clip(relative * inverse_floor - 1.0, 0.0, 1.0)


def probability_kernel(every_ref, share_ref, top_ref, floor_ref, out_ref):
    mine, vocab = share_ref.shape
    devices, lines, _ = every_ref.shape
    part = vocab * mine // lines
    inverse = FIXED_POINT / floor_ref[:, 0:1].astype(f32)
    tops = [
        jnp.sum(every_ref[device, :, part:].astype(f32), axis=1, keepdims=True)
        for device in range(devices)
    ]
    peak = functools.reduce(jnp.maximum, tops)
    per_row = lines // mine
    spread = jnp.concatenate(
        [jnp.broadcast_to(inverse[row : row + 1], (per_row, 1)) for row in range(mine)], axis=0
    )
    kept = jnp.zeros((lines, part), f32)
    for device in range(devices):
        relative = every_ref[device, :, :part].astype(f32) * jnp.exp(tops[device] - peak)
        kept = kept + weigh(relative, spread)
    kept = jnp.sum(kept, axis=1, keepdims=True)
    total = jnp.concatenate(
        [jnp.sum(kept[row * per_row : (row + 1) * per_row], axis=0, keepdims=True) for row in range(mine)],
        axis=0,
    )
    highest = jnp.concatenate([peak[row * per_row : row * per_row + 1] for row in range(mine)], axis=0)
    own = weigh(share_ref[...] * jnp.exp(top_ref[:, 0:1] - highest), inverse)
    out_ref[...] = (own / total).astype(bf16)


def regroup_matrix(ref):
    columns = ref.shape[0]
    source = lax.broadcasted_iota(jnp.int32, ref.shape, 0)
    target = lax.broadcasted_iota(jnp.int32, ref.shape, 1)
    order = (source % GROUPS) * (columns // GROUPS) + source // GROUPS == target
    ref[...] = order.astype(f32).astype(bf16)


def head_matrix(ref):
    head = lax.broadcasted_iota(jnp.int32, ref.shape, 0)
    channel = lax.broadcasted_iota(jnp.int32, ref.shape, 1)
    ref[...] = (channel // HEAD_DIM == head).astype(f32).astype(bf16)


def fetch_kernel(count, jobs, makes, *refs):
    sources = refs[:count]
    targets = refs[count + 1 : count + 1 + len(jobs)]
    made = refs[count + 1 + len(jobs) : -1]
    sems = refs[-1]
    copies = []
    for (at, kind, start), target in zip(jobs, targets):
        if kind == "whole":
            moves = [(sources[at], target)]
        elif kind == "columns":
            moves = [(sources[at].at[:, pl.ds(start, target.shape[1])], target)]
        else:
            moves = tile_moves(sources[at], start, target, 1)
        for source, place in moves:
            copies.append(pltpu.make_async_copy(source, place, sems.at[len(copies)]))
    for copy in copies:
        copy.start()
    if makes:

        @beside_copies
        def _():
            for make, ref in zip(makes, made):
                make(ref)

    for copy in copies:
        copy.wait()


def fetch(jobs, after, name, makes=()):
    jobs = [job for job in jobs if 0 not in job[3]]
    if not jobs and not makes:
        return []
    sources = []
    for source, *_ in jobs:
        if not any(source is other for other in sources):
            sources.append(source)
    plan = [
        ([source is other for other in sources].index(True), kind, start) for source, kind, start, _ in jobs
    ]
    outs = [pltpu.VMEM(dims, bf16) for *_, dims in jobs] + [pltpu.VMEM(dims, bf16) for _, dims in makes]
    size = sum(2 * functools.reduce(lambda a, b: a * b, dims) for *_, dims in jobs)
    return list(call(
        functools.partial(fetch_kernel, len(sources), plan, [make for make, _ in makes]),
        outs,
        [in_hbm(source) for source in sources] + [after],
        [ANY] * (len(sources) + 1),
        scratch=[pltpu.SemaphoreType.DMA((sum(dims[0] if kind == "tiles" else 1 for _, kind, _, dims in jobs),))],
        limit=2,
        cost=1000,
        out_specs=[VMEM] * len(outs),
        name=name,
    ))


def local(
    hidden,
    norm_gain,
    input_weight,
    group_weight,
    step_weight,
    conv_inner_weight,
    conv_group_weight,
    conv_inner_state,
    conv_group_state,
    timestep_bias,
    decay_log,
    skip_gain,
    recurrent_state,
    mixer_gain,
    output_weight,
    final_gain,
    lexicon_matrix,
    token_mask,
    min_share,
):
    mine, heads_mine, head_width, state_width = recurrent_state.shape
    width = heads_mine * head_width
    rows, depth = hidden.shape
    vocab = lexicon_matrix.shape[1]
    row_devices = lax.axis_size("row")
    head_devices = lax.axis_size("head")
    group_devices = head_devices // GROUPS
    columns = group_weight.shape[1]
    entries = columns // GROUPS
    held_rows = 8

    heads = jnp.pad(
        jnp.stack([timestep_bias, decay_log, skip_gain]), ((0, 0), (0, LANES - heads_mine))
    )
    inner_state = jnp.moveaxis(conv_inner_state, 1, 0)
    group_state = jnp.moveaxis(conv_group_state, 1, 0)
    state = recurrent_state.reshape(mine, width, state_width)
    floors = jnp.broadcast_to(min_share[:, None], (mine, LANES))

    kept_arrays = [hidden, norm_gain.reshape(-1, LANES), step_weight.T]
    used_arrays = [group_weight, group_state, conv_group_weight]
    hidden_held, gain_held, step_held, group_part, squares, sent = call(
        functools.partial(group_kernel, len(kept_arrays)),
        [pltpu.VMEM(array.shape, array.dtype) for array in kept_arrays]
        + [
            shape((rows, columns)),
            shape((rows, LANES)),
            shape((head_devices, rows + held_rows, 2 * entries), bf16),
        ],
        [in_hbm(array) for array in kept_arrays + used_arrays],
        [ANY] * 6,
        scratch=[pltpu.VMEM((columns, columns), bf16)]
        + [pltpu.VMEM(array.shape, array.dtype) for array in used_arrays]
        + [
            pltpu.VMEM((2 * rows + 2 * held_rows, columns), f32),
            pltpu.SemaphoreType.DMA((6,)),
        ],
        limit=6,
        cost=2 * MIB,
        out_specs=[VMEM] * 6,
        name="group_projection",
    )
    arrived = lax.all_to_all(sent, "head", 0, 0, tiled=True)
    all_squares = [squares] + [row_send(squares, at) for at in range(1, row_devices)]
    pairs = width // TILE
    early = 2 * (pairs * EARLY_INPUT // 8)
    late = width // LANES - early
    input_held = fetch(
        [(input_weight, "tiles", at, (2, 2 * depth, LANES)) for at in range(0, early, 2)],
        arrived,
        "fetch_input",
    )
    parts = 1
    both, small = call(
        functools.partial(input_kernel, row_devices, len(input_held)),
        [shape((2 * rows, width)), shape((rows, 2 * LANES))],
        all_squares + [hidden_held, gain_held, step_held] + input_held + [in_hbm(input_weight)],
        [VMEM] * (row_devices + 3 + len(input_held)) + [ANY],
        scratch=[
            pltpu.VMEM((2 * rows, 2 * depth), bf16),
            pltpu.VMEM((late, 2 * depth, LANES), bf16),
            pltpu.SemaphoreType.DMA((late * parts,)),
        ],
        limit=late + 6,
        cost=2 * input_weight.size,
        name="input_projection",
    )
    tiles = vocab // TILE
    cuts = [tiles * share // 32 * TILE for share in SHARES]
    spans = [(start, end - start) for start, end in zip([0] + cuts[:-1], cuts)]
    fetched = []

    def lexicon_job(stage):
        start, size = spans[stage]
        return (lexicon_matrix, "columns", start, (depth, size))

    def fetch_lexicon(stage, after, name):
        if not spans[stage][1]:
            return after
        fetched.extend(fetch([lexicon_job(stage)], after, name))
        return fetched[-1]

    packed_width = 2 * width + columns + LANES + 2 * state_width
    packed, held = call(
        pack_kernel,
        [shape((row_devices, mine, packed_width)), shape((2, held_rows, 2 * state_width))],
        [both, group_part, small, arrived],
        [VMEM] * 4,
        cost=16 * MIB,
        name="pack_rows",
    )
    pieces = [packed[0]] + [row_send(packed[at], at) for at in range(1, row_devices)]

    *fetched, spread = fetch(
        [lexicon_job(0)],
        packed,
        "fetch_lexicon_0",
        [(head_matrix, (LANES, width))],
    )
    finish = group_devices == 1
    mixer_in, raw, driven, decay, state_input = call(
        functools.partial(state_kernel, finish, row_devices),
        [
            shape((mine, width), bf16 if finish else f32),
            shape((mine, width + columns)),
            shape((mine, width)),
            shape((mine, width)),
            shape((mine, state_width)),
        ],
        pieces + [heads, held, inner_state, conv_inner_weight, state, mixer_gain[None], spread],
        [VMEM] * (row_devices + 7),
        limit=8,
        cost=1000,
        name="state_readout",
    )
    if not finish:
        members = [
            [group * group_devices + at for at in range(group_devices)] for group in range(GROUPS)
        ]
        group_total = lax.psum(jnp.sum(mixer_in * mixer_in, axis=1), "head", axis_index_groups=members)
        group_scale = lax.rsqrt(group_total / (HEADS * HEAD_DIM // GROUPS) + EPSILON)
        mixer_in = (mixer_in * group_scale[:, None] * mixer_gain.astype(f32)[None]).astype(bf16)

    mixer_rows = [mixer_in] + [row_send(mixer_in, at) for at in range(1, row_devices)]
    ahead = fetch_lexicon(1, mixer_in, "fetch_lexicon_1")
    mixed = call(
        functools.partial(output_kernel, row_devices),
        shape((rows, depth)),
        mixer_rows + [output_weight, ahead],
        [VMEM] * (row_devices + 1) + [ANY],
        scratch=[pltpu.VMEM((row_devices, mine, width), f32)],
        cost=1000,
        name="output_projection",
    )
    distance, stage = 1, 2
    while distance < head_devices:
        steps = [distance]
        if distance > 1 and 4 * distance <= head_devices:
            steps = [distance, 2 * distance, 3 * distance]
        others = [xor_permute(mixed, "head", step) for step in steps]
        ahead = mixed
        if distance > 1 and stage < len(SHARES):
            ahead = fetch_lexicon(stage, mixed, f"fetch_lexicon_{stage}")
            stage += 1
        mixed = call(
            functools.partial(add_kernel, 1 + len(steps)),
            shape((rows, depth)),
            [mixed] + others + [ahead],
            [VMEM] * (1 + len(steps)) + [ANY],
            name="add",
        )
        distance *= 1 + len(steps)
    layer, scores = call(
        functools.partial(lexicon_kernel, len(fetched)),
        [pltpu.VMEM((rows, depth), bf16), shape((row_devices, mine, vocab + LANES), jnp.int16)],
        [hidden_held, final_gain[None], mixed] + fetched + [in_hbm(lexicon_matrix)],
        [VMEM] * (3 + len(fetched)) + [ANY],
        scratch=[
            pltpu.VMEM((depth, vocab - cuts[-1]), bf16),
            pltpu.VMEM((2 * rows, depth), bf16),
            pltpu.VMEM((rows, vocab + LANES), f32),
            pltpu.SemaphoreType.DMA((max(1, (vocab - cuts[-1]) // (2 * TILE)),)),
        ],
        limit=16,
        cost=16 * MIB,
        name="lexicon_projection",
    )
    score_rows = [scores[0]] + [row_send(scores[at], at) for at in range(1, row_devices)]
    next_state, next_inner, next_group, layer_out = call(
        update_kernel,
        [
            shape((mine, width, state_width), bf16),
            shape((3, mine, width), bf16),
            shape((3, mine, columns), bf16),
            shape((rows, depth), bf16),
        ],
        [driven, decay, state_input, state, raw, inner_state, group_state, layer, scores],
        [VMEM] * 8 + [ANY],
        scratch=[
            pltpu.VMEM((mine, width, state_width), bf16),
            pltpu.SemaphoreType.DMA((mine, width // min(512, width))),
        ],
        limit=8,
        cost=4 * MIB,
        out_specs=[ANY, VMEM, VMEM, VMEM],
        name="state_update",
    )
    lines = 8 * mine
    shares, share, top = call(
        functools.partial(share_kernel, row_devices),
        [
            shape((lines, vocab * mine // lines + LANES), bf16),
            shape((mine, vocab)),
            shape((mine, LANES)),
        ],
        score_rows + [token_mask],
        [VMEM] * (row_devices + 1),
        scratch=[pltpu.VMEM((lines, vocab * mine // lines + LANES), f32)],
        name="share_of_peak",
    )
    every = lax.all_gather(shares, "head", axis=0)
    next_probs = call(
        probability_kernel,
        shape((mine, vocab), bf16),
        [every, share, top, floors],
        [VMEM] * 4,
        name="probabilities",
    )
    return (
        next_state.reshape(recurrent_state.shape),
        jnp.moveaxis(next_inner, 0, 1),
        jnp.moveaxis(next_group, 0, 1),
        layer_out,
        next_probs,
    )


def solution(mesh):
    in_specs = (
        P(None, "row"),
        P("row"),
        P("row", None, "head"),
        P("row", "head"),
        P("row", "head"),
        P(None, "head"),
        P(None, "head"),
        P("row", None, "head"),
        P("row", None, "head"),
        P("head"),
        P("head"),
        P("head"),
        P("row", "head", None, None),
        P("head"),
        P("head", "row"),
        P("row"),
        P("row", "head"),
        P("row", "head"),
        P("row"),
    )
    out_specs = (
        P("row", "head", None, None),
        P("row", None, "head"),
        P("row", None, "head"),
        P(None, "row"),
        P("row", "head"),
    )
    return jax.shard_map(local, mesh=mesh, in_specs=in_specs, out_specs=out_specs, check_vma=False)
```

```python
import functools

import jax
import jax.numpy as jnp
from jax import lax
from jax.experimental import pallas as pl
from jax.experimental.pallas import tpu as pltpu
from jax.sharding import PartitionSpec as P

D = 8192
HEADS = 256
HEAD_DIM = 64
GROUPS = 8
FIXED_BITS = 15.0

EPSILON = 1e-05
INVERSE_HEAT = 1.25
FIXED_POINT = 65536.0
NEG_LARGE = -1e30

MIB = 2**20
LANES = 128
TILE = 256
SHARES = (4, 12, 22)
EARLY_INPUT = 5
VMEM = pl.BlockSpec(memory_space=pltpu.VMEM)
ANY = pl.BlockSpec(memory_space=pl.ANY)
f32 = jnp.float32
bf16 = jnp.bfloat16


def xor_permute(values, axis, distance):
    size = lax.axis_size(axis)
    return lax.ppermute(values, axis, [(at, at ^ distance) for at in range(size)])


def row_send(values, distance):
    size = lax.axis_size("row")
    return lax.ppermute(values, "row", [(at, (at + distance) % size) for at in range(size)])


def row_place(block, index, count):
    return lax.rem(block - index + count, count)


def row_origin(index, distance, count):
    return lax.rem(index - distance + count, count)


def tree_sum(values):
    values = list(values)
    while len(values) > 1:
        values = [a + b for a, b in zip(values[0::2], values[1::2])]
    return values[0]


def split(values):
    high = values.astype(bf16)
    return high, (values - high.astype(f32)).astype(bf16)


def split_three(values):
    high, rest = split(values)
    middle = values - high.astype(f32)
    return high, rest, (middle - rest.astype(f32)).astype(bf16)


def silu(values):
    return values / (1.0 + jnp.exp(-values))


def dot(left, right):
    return jnp.dot(left, right, preferred_element_type=f32)


def dot_transposed(left, right):
    return lax.dot_general(left, right, (((1,), (1,)), ((), ())), preferred_element_type=f32)


def times_gain(values, gain_ref):
    return jnp.concatenate(
        [
            values[:, at * LANES : (at + 1) * LANES] * gain_ref[at : at + 1].astype(f32)
            for at in range(gain_ref.shape[0])
        ],
        axis=1,
    )


def beside_copies(body):
    pl.when(lax.axis_index("row") >= 0)(body)


def in_hbm(values):
    return pltpu.with_memory_space_constraint(values, pltpu.HBM)


def call(kernel, outs, operands, specs, scratch=(), limit=4, cost=0, out_specs=None, name=None):
    return pl.pallas_call(
        kernel,
        out_shape=outs,
        in_specs=specs,
        out_specs=out_specs if out_specs is not None else jax.tree.map(lambda _: VMEM, outs),
        scratch_shapes=list(scratch),
        compiler_params=pltpu.CompilerParams(vmem_limit_bytes=limit * MIB),
        cost_estimate=pl.CostEstimate(flops=1000, bytes_accessed=cost, transcendentals=0),
        name=name,
    )(*operands)


def shape(dims, dtype=f32):
    return jax.ShapeDtypeStruct(tuple(dims), dtype)


def group_kernel(keep, *refs):
    sources = refs[: keep + 3]
    weight_hbm, state_hbm, taps_hbm = sources[keep:]
    kept = refs[keep + 3 : 2 * keep + 3]
    part_ref, squares_ref, sent_ref, order, weight_ref, state_ref, taps_ref, stack, sems = refs[2 * keep + 3 :]
    places = list(kept) + [weight_ref, state_ref, taps_ref]
    copies = [
        pltpu.make_async_copy(source, place, sems.at[at])
        for at, (source, place) in enumerate(zip(sources, places))
    ]
    for copy in copies:
        copy.start()

    @beside_copies
    def _():
        regroup_matrix(order)
        stack[...] = jnp.zeros_like(stack)

    hidden_ref, gain_ref = kept[:2]
    rows = hidden_ref.shape[0]
    columns = weight_ref.shape[1]
    entries = columns // GROUPS
    devices = sent_ref.shape[0]
    for copy in copies:
        copy.wait()
    wide = hidden_ref[...].astype(f32)
    squares_ref[...] = jnp.broadcast_to(jnp.sum(wide * wide, axis=1, keepdims=True), squares_ref.shape)
    high, low = split(times_gain(wide, gain_ref))
    part = dot(jnp.concatenate([high, low], axis=0), weight_ref[...])
    part = part[:rows] + part[rows:]
    part_ref[...] = part
    part_high, part_low = split(part)
    stack[:rows] = part_high.astype(f32)
    stack[rows : 2 * rows] = part_low.astype(f32)
    taps = taps_ref[...].astype(f32)
    for side in range(2):
        here = 2 * rows + 8 * side
        for at in range(3):
            stack[here + at : here + at + 1] = state_ref[at, side : side + 1].astype(f32)
        for at in range(2):
            stack[here + 3 + at : here + 4 + at] = taps[2 * at + side : 2 * at + side + 1]
    grouped = dot(stack[...].astype(bf16), order[...])
    each = devices // GROUPS
    for group in range(GROUPS):
        here = grouped[:, group * entries : (group + 1) * entries]
        first = jnp.concatenate([here[:rows], here[2 * rows : 2 * rows + 8]], axis=0)
        second = jnp.concatenate([here[rows : 2 * rows], here[2 * rows + 8 :]], axis=0)
        value = jnp.concatenate([first, second], axis=1).astype(bf16)
        for at in range(each):
            sent_ref[group * each + at] = value


def input_tile(weight_ref, at):
    depth, _, width = weight_ref.shape
    return weight_ref.reshape(2 * depth, width).at[:, pl.ds(at * LANES, LANES)]


def tile_moves(weight_ref, start, target, parts):
    size = target.shape[1] // parts
    return [
        (input_tile(weight_ref, start + tile).at[pl.ds(at * size, size)], target.at[tile, pl.ds(at * size, size)])
        for tile in range(target.shape[0])
        for at in range(parts)
    ]


def input_kernel(pieces, count, *refs):
    square_refs = refs[:pieces]
    hidden_ref, gain_ref, step_ref = refs[pieces : pieces + 3]
    tiles = list(refs[pieces + 3 : pieces + 3 + count])
    weight_ref, out_ref, small_ref, left, rest, sems = refs[pieces + 3 + count :]
    depth, _, width = weight_ref.shape
    rows = hidden_ref.shape[0]
    held = 2 * count
    parts = sems.shape[0] // rest.shape[0]
    copies = [
        pltpu.make_async_copy(source, place, sems.at[at])
        for at, (source, place) in enumerate(tile_moves(weight_ref, held, rest, parts))
    ]
    for copy in copies:
        copy.start()
    def project(first, pair):
        out_ref[:, first * LANES : (first + 2) * LANES] = dot(left[...], jnp.concatenate(pair, axis=1))

    @beside_copies
    def _():
        squares = tree_sum([ref[...] for ref in square_refs])[:, 0:1]
        scale = lax.rsqrt(squares / D + EPSILON)
        normed = times_gain(hidden_ref[...].astype(f32) * scale, gain_ref).astype(bf16).astype(f32)
        step = dot_transposed(normed.astype(bf16), step_ref[...])
        small_ref[...] = jnp.zeros_like(small_ref)
        small_ref[:, : step.shape[1]] = step
        small_ref[:, LANES:] = jnp.broadcast_to(scale, (rows, LANES))
        source = lax.broadcasted_iota(jnp.int32, (LANES, 4 * LANES), 0)
        target = lax.broadcasted_iota(jnp.int32, (LANES, 4 * LANES), 1)
        spread = 2 * source + target // (2 * LANES) == target % (2 * LANES)
        blocks = jnp.concatenate(
            [normed[:, block * LANES : (block + 1) * LANES] for block in range(depth // LANES)], axis=0
        )
        wide = dot(blocks.astype(bf16), spread.astype(f32).astype(bf16))
        for block in range(depth // LANES):
            here = wide[block * rows : (block + 1) * rows]
            left[:, 2 * block * LANES : 2 * (block + 1) * LANES] = jnp.concatenate(
                [here[:, : 2 * LANES], here[:, 2 * LANES :]], axis=0
            ).astype(bf16)
        for first in range(0, held, 2):
            project(first, [tiles[first // 2][0], tiles[first // 2][1]])

    for first in range(held, width // LANES, 2):
        for copy in copies[(first - held) * parts : (first - held + 2) * parts]:
            copy.wait()
        project(first, [rest[first - held], rest[first - held + 1]])


def fixed_exponent(values):
    return jnp.floor(jnp.log2(jnp.maximum(values, 1e-30))) + 2.0


def pack_kernel(both_ref, part_ref, small_ref, arrived_ref, out_ref, held_ref, joined):
    rows, width = small_ref.shape[0], both_ref.shape[1]
    blocks, mine, _ = out_ref.shape
    devices, _, double = arrived_ref.shape
    entries = double // 2
    columns = part_ref.shape[1]
    index = lax.axis_index("row")
    scale = small_ref[:, LANES : LANES + 1]
    arrived = arrived_ref[...].astype(f32)
    pair = (arrived[:, :rows, :entries] + arrived[:, :rows, entries:]) * scale[None]
    part = part_ref[...] * scale
    held_ref[...] = jnp.zeros_like(held_ref)
    for device in range(devices):
        here = slice(device * entries, (device + 1) * entries)
        for side in range(2):
            lines = arrived[device, rows:, side * entries : (side + 1) * entries]
            for at in range(3):
                held_ref[0, at * mine + side : at * mine + side + 1, here] = lines[at : at + 1]
            for at in range(2):
                held_ref[1, 2 * at + side : 2 * at + side + 1, here] = lines[3 + at : 4 + at]
    for device in range(devices):
        joined[:, device * entries : (device + 1) * entries] = pair[device]
    sections = [both_ref[:rows], both_ref[rows:], part, small_ref[:, :LANES], joined[...]]
    lane = lax.broadcasted_iota(jnp.int32, (rows, LANES), 1)
    tail = jnp.zeros((rows, LANES), f32)
    start = 0

    def put(value, start):
        value = value.astype(jnp.int32).astype(jnp.int16)
        for block in range(blocks):
            here = value[block * mine : (block + 1) * mine]
            out_ref[row_place(block, index, blocks), :, start : start + value.shape[1]] = here

    for at, value in enumerate(sections):
        exponent = fixed_exponent(jnp.max(jnp.abs(value), axis=1, keepdims=True))
        tail = jnp.where(lane == at, exponent, tail)
        put(jnp.round(value * jnp.exp2(FIXED_BITS - exponent)), start)
        start += value.shape[1]
    put(tail, start)


def state_kernel(finish, pieces, *refs):
    heads_ref, held_ref, inner_state_ref, inner_taps_ref = refs[pieces : pieces + 4]
    state_ref, gain_ref, spread_ref = refs[pieces + 4 : pieces + 7]
    mixer_ref, raw_ref, driven_ref, decay_ref, input_ref = refs[pieces + 7 :]
    mine, width, state_width = state_ref.shape
    columns = raw_ref.shape[1] - width
    widths = [width, width, columns, LANES, 2 * state_width]
    length = sum(widths)
    tails = [ref[:, length:].astype(jnp.int32).astype(f32) for ref in refs[:pieces]]
    sections, start = [], 0
    for at, size in enumerate(widths):
        sections.append(
            tree_sum(
                ref[:, start : start + size].astype(jnp.int32).astype(f32)
                * jnp.exp2(tail[:, at : at + 1] - FIXED_BITS)
                for ref, tail in zip(refs[:pieces], tails)
            )
        )
        start += size
    gate, inner_sum, group_sum, step_sum, pair_sum = sections
    inner_raw = inner_sum.astype(bf16)
    raw_ref[:, :width] = inner_sum
    raw_ref[:, width:] = group_sum
    taps = inner_taps_ref[...].astype(f32)
    mixed = inner_raw.astype(f32) * taps[3:4]
    for at in range(3):
        mixed = mixed + inner_state_ref[at].astype(f32) * taps[at : at + 1]
    conv_inner = silu(mixed)
    taps = held_ref[1]
    mixed = pair_sum.astype(bf16).astype(f32) * taps[3:4]
    for at in range(3):
        mixed = mixed + held_ref[0, at * mine : (at + 1) * mine] * taps[at : at + 1]
    pair = silu(mixed).astype(bf16)
    state_input = pair[:, :state_width].astype(f32)
    state_output = pair[:, state_width:]

    step_raw = step_sum + heads_ref[0:1]
    step_size = jnp.maximum(step_raw, 0.0) + jnp.log1p(jnp.exp(-jnp.abs(step_raw)))
    decay_rate = jnp.exp(-step_size * jnp.exp(heads_ref[1:2]))
    stacked = jnp.concatenate([step_size, decay_rate, heads_ref[2:3]], axis=0)
    parts = split_three(stacked)
    wide = (dot(parts[0], spread_ref[...]) + dot(parts[1], spread_ref[...])) + dot(parts[2], spread_ref[...])
    step_wide, decay_wide, skip_wide = wide[:mine], wide[mine : 2 * mine], wide[2 * mine :]
    driven = step_wide * conv_inner
    overlap = jnp.sum(state_input * state_output.astype(f32), axis=1, keepdims=True)
    old = jnp.concatenate(
        [dot_transposed(state_output, state_ref[row])[row : row + 1] for row in range(mine)], axis=0
    )
    readout = decay_wide * old + driven * overlap + skip_wide * conv_inner
    gated = readout * silu(gate)
    driven_ref[...] = driven
    decay_ref[...] = decay_wide
    input_ref[...] = state_input
    if finish:
        group_total = jnp.sum(gated * gated, axis=1, keepdims=True)
        group_scale = lax.rsqrt(group_total / (HEADS * HEAD_DIM // GROUPS) + EPSILON)
        gated = gated * group_scale * gain_ref[...].astype(f32)
    mixer_ref[...] = gated.astype(mixer_ref.dtype)


def update_kernel(
    driven_ref, decay_ref, input_ref, state_ref, raw_ref, inner_state_ref, group_state_ref, layer_ref, _, *refs
):
    out_ref, next_inner_ref, next_group_ref, layer_out_ref, new, sems = refs
    mine, width, _ = state_ref.shape
    block = min(512, width)
    blocks = width // block

    def copy(row, at):
        here = pl.ds(at * block, block)
        return pltpu.make_async_copy(new.at[row, here], out_ref.at[row, here], sems.at[row, at])

    for row in range(mine):
        both = jnp.concatenate(
            [driven_ref[row : row + 1], decay_ref[row : row + 1], jnp.zeros((6, width), f32)], axis=0
        )
        turned = jnp.transpose(both)
        for at in range(blocks):
            here = slice(at * block, (at + 1) * block)
            new[row, here] = (
                turned[here, 1:2] * state_ref[row, here].astype(f32)
                + turned[here, 0:1] * input_ref[row : row + 1]
            ).astype(bf16)
            copy(row, at).start()
    layer_out_ref[...] = layer_ref[...]
    next_inner_ref[0] = inner_state_ref[1]
    next_inner_ref[1] = inner_state_ref[2]
    next_inner_ref[2] = raw_ref[:, :width].astype(bf16)
    next_group_ref[0] = group_state_ref[1]
    next_group_ref[1] = group_state_ref[2]
    next_group_ref[2] = raw_ref[:, width:].astype(bf16)
    for row in range(mine):
        for at in range(blocks):
            copy(row, at).wait()


def output_kernel(pieces, *refs):
    weight_ref, _, out_ref, rows_held = refs[pieces:]
    index = lax.axis_index("row")
    for at in range(pieces):
        rows_held[row_origin(index, at, pieces)] = refs[at][...].astype(f32)
    left = jnp.concatenate([rows_held[at] for at in range(pieces)], axis=0).astype(bf16)
    width = weight_ref.shape[1]
    for column in range(0, width, TILE):
        out_ref[:, column : column + TILE] = dot(left, weight_ref[:, column : column + TILE])


def plain(ref):
    if ref.dtype != jnp.int16:
        return ref[...]
    width = ref.shape[1] - LANES
    tail = ref[:, width:].astype(jnp.int32).astype(f32)
    return ref[:, :width].astype(jnp.int32).astype(f32) * jnp.exp2(tail[:, 0:1] - FIXED_BITS)


def encode_kernel(*refs):
    value = tree_sum([plain(ref) for ref in refs[:-1]])
    width = value.shape[1]
    exponent = fixed_exponent(jnp.max(jnp.abs(value), axis=1, keepdims=True))
    digits = jnp.round(value * jnp.exp2(FIXED_BITS - exponent))
    refs[-1][:, :width] = digits.astype(jnp.int32).astype(jnp.int16)
    tail = jnp.broadcast_to(exponent, (value.shape[0], LANES))
    refs[-1][:, width:] = tail.astype(jnp.int32).astype(jnp.int16)


def lexicon_kernel(terms, pieces, *refs):
    hidden_ref, gain_ref = refs[:2]
    mixed_refs = refs[2 : 2 + terms]
    held_refs = refs[2 + terms : 2 + terms + pieces]
    weight_ref, layer_ref, out_ref, rest, left, scores, sems = refs[2 + terms + pieces :]
    rows = hidden_ref.shape[0]
    blocks, mine, _ = out_ref.shape
    vocab = weight_ref.shape[1]
    done = vocab - rest.shape[1]
    part = rest.shape[1] // sems.shape[0]
    copies = [
        pltpu.make_async_copy(
            weight_ref.at[:, pl.ds(done + at * part, part)], rest.at[:, pl.ds(at * part, part)], sems.at[at]
        )
        for at in range(sems.shape[0])
    ]
    for copy in copies:
        copy.start()
    index = lax.axis_index("row")

    def put(value, column, width):
        value = value.astype(jnp.int32).astype(jnp.int16)
        for block in range(blocks):
            out_ref[row_place(block, index, blocks), :, column : column + width] = value[block * mine : (block + 1) * mine]

    def project(tile, column):
        term = dot(left[...], tile)
        scores[:, column : column + TILE] = term[:rows] + term[rows:]

    @beside_copies
    def _():
        mixed = tree_sum([plain(ref) for ref in mixed_refs])
        layer = (hidden_ref[...].astype(f32) + mixed).astype(bf16)
        layer_ref[...] = layer
        wide = layer.astype(f32)
        squares = jnp.sum(wide * wide, axis=1, keepdims=True)
        high, low = split(wide * gain_ref[...].astype(f32))
        left[:rows] = high
        left[rows:] = low
        scores[:, vocab:] = jnp.broadcast_to(squares, (rows, LANES))
        base = 0
        for held in held_refs:
            for column in range(0, held.shape[1], TILE):
                project(held[:, column : column + TILE], base + column)
            base += held.shape[1]

    for column in range(0, rest.shape[1], TILE):
        if column % part == 0:
            copies[column // part].wait()
        project(rest[:, column : column + TILE], done + column)
    squares = scores[:, vocab : vocab + 1]
    peak = jnp.max(jnp.abs(scores[:, :vocab]), axis=1, keepdims=True)
    exponent = fixed_exponent(peak)
    square_exponent = fixed_exponent(squares)
    digits = squares * jnp.exp2(FIXED_BITS - square_exponent)
    digit = jnp.floor(digits)
    rest_digit = jnp.floor((digits - digit) * 2.0**FIXED_BITS)
    lane = lax.broadcasted_iota(jnp.int32, (rows, LANES), 1)
    tail = jnp.where(lane == 0, exponent, jnp.where(lane == 1, square_exponent, 0.0))
    put(jnp.where(lane == 2, digit, jnp.where(lane == 3, rest_digit, tail)), vocab, LANES)
    factor = jnp.exp2(FIXED_BITS - exponent)
    for column in range(0, vocab, 4 * TILE):
        put(jnp.round(scores[:, column : column + 4 * TILE] * factor), column, 4 * TILE)


def share_kernel(pieces, *refs):
    mask_ref, sent_ref, share_ref, top_ref, spread = refs[pieces:]
    mine, vocab = mask_ref.shape
    lines = sent_ref.shape[0] // mine
    part = vocab // lines
    terms, squares = [], []
    for ref in refs[:pieces]:
        tail = ref[:, vocab:].astype(jnp.int32).astype(f32)
        digits = tail[:, 2:3] + tail[:, 3:4] * 2.0**-FIXED_BITS
        squares.append(digits * jnp.exp2(tail[:, 1:2] - FIXED_BITS))
        terms.append(ref[:, :vocab].astype(jnp.int32).astype(f32) * jnp.exp2(tail[:, 0:1] - FIXED_BITS))
    scale = lax.rsqrt(tree_sum(squares) / D + EPSILON) * INVERSE_HEAT
    allowed = mask_ref[...] > 0
    logits = jnp.where(allowed, tree_sum(terms) * scale, NEG_LARGE)
    top = jnp.max(logits, axis=1, keepdims=True)
    share = jnp.where(allowed, jnp.exp(logits - top), 0.0)
    share_ref[...] = share
    top_ref[...] = jnp.broadcast_to(top, top_ref.shape)
    spread[...] = jnp.zeros_like(spread)
    parts = [value.astype(f32) for value in split_three(top)]
    for row in range(mine):
        for line in range(lines):
            here = slice(row * lines + line, row * lines + line + 1)
            spread[here, :part] = share[row : row + 1, line * part : (line + 1) * part]
        here = slice(row * lines, (row + 1) * lines)
        for at in range(3):
            spread[here, part + at : part + at + 1] = jnp.broadcast_to(parts[at][row : row + 1], (lines, 1))
    sent_ref[...] = spread[...].astype(bf16)


def weigh(relative, inverse_floor):
    return relative * jnp.clip(relative * inverse_floor - 1.0, 0.0, 1.0)


def probability_kernel(every_ref, share_ref, top_ref, floor_ref, out_ref):
    mine, vocab = share_ref.shape
    devices, lines, _ = every_ref.shape
    part = vocab * mine // lines
    inverse = FIXED_POINT / floor_ref[:, 0:1].astype(f32)
    tops = [
        jnp.sum(every_ref[device, :, part:].astype(f32), axis=1, keepdims=True)
        for device in range(devices)
    ]
    peak = functools.reduce(jnp.maximum, tops)
    per_row = lines // mine
    spread = jnp.concatenate(
        [jnp.broadcast_to(inverse[row : row + 1], (per_row, 1)) for row in range(mine)], axis=0
    )
    kept = jnp.zeros((lines, part), f32)
    for device in range(devices):
        relative = every_ref[device, :, :part].astype(f32) * jnp.exp(tops[device] - peak)
        kept = kept + weigh(relative, spread)
    kept = jnp.sum(kept, axis=1, keepdims=True)
    total = jnp.concatenate(
        [jnp.sum(kept[row * per_row : (row + 1) * per_row], axis=0, keepdims=True) for row in range(mine)],
        axis=0,
    )
    highest = jnp.concatenate([peak[row * per_row : row * per_row + 1] for row in range(mine)], axis=0)
    own = weigh(share_ref[...] * jnp.exp(top_ref[:, 0:1] - highest), inverse)
    out_ref[...] = (own / total).astype(bf16)


def regroup_matrix(ref):
    columns = ref.shape[0]
    source = lax.broadcasted_iota(jnp.int32, ref.shape, 0)
    target = lax.broadcasted_iota(jnp.int32, ref.shape, 1)
    order = (source % GROUPS) * (columns // GROUPS) + source // GROUPS == target
    ref[...] = order.astype(f32).astype(bf16)


def head_matrix(ref):
    head = lax.broadcasted_iota(jnp.int32, ref.shape, 0)
    channel = lax.broadcasted_iota(jnp.int32, ref.shape, 1)
    ref[...] = (channel // HEAD_DIM == head).astype(f32).astype(bf16)


def fetch_kernel(count, jobs, makes, *refs):
    sources = refs[:count]
    targets = refs[count + 1 : count + 1 + len(jobs)]
    made = refs[count + 1 + len(jobs) : -1]
    sems = refs[-1]
    copies = []
    for (at, kind, start), target in zip(jobs, targets):
        if kind == "whole":
            moves = [(sources[at], target)]
        elif kind == "columns":
            moves = [(sources[at].at[:, pl.ds(start, target.shape[1])], target)]
        else:
            moves = tile_moves(sources[at], start, target, 1)
        for source, place in moves:
            copies.append(pltpu.make_async_copy(source, place, sems.at[len(copies)]))
    for copy in copies:
        copy.start()
    if makes:

        @beside_copies
        def _():
            for make, ref in zip(makes, made):
                make(ref)

    for copy in copies:
        copy.wait()


def fetch(jobs, after, name, makes=()):
    jobs = [job for job in jobs if 0 not in job[3]]
    if not jobs and not makes:
        return []
    sources = []
    for source, *_ in jobs:
        if not any(source is other for other in sources):
            sources.append(source)
    plan = [
        ([source is other for other in sources].index(True), kind, start) for source, kind, start, _ in jobs
    ]
    outs = [pltpu.VMEM(dims, bf16) for *_, dims in jobs] + [pltpu.VMEM(dims, bf16) for _, dims in makes]
    size = sum(2 * functools.reduce(lambda a, b: a * b, dims) for *_, dims in jobs)
    return list(call(
        functools.partial(fetch_kernel, len(sources), plan, [make for make, _ in makes]),
        outs,
        [in_hbm(source) for source in sources] + [after],
        [ANY] * (len(sources) + 1),
        scratch=[pltpu.SemaphoreType.DMA((sum(dims[0] if kind == "tiles" else 1 for _, kind, _, dims in jobs),))],
        limit=2,
        cost=1000,
        out_specs=[VMEM] * len(outs),
        name=name,
    ))


def local(
    hidden,
    norm_gain,
    input_weight,
    group_weight,
    step_weight,
    conv_inner_weight,
    conv_group_weight,
    conv_inner_state,
    conv_group_state,
    timestep_bias,
    decay_log,
    skip_gain,
    recurrent_state,
    mixer_gain,
    output_weight,
    final_gain,
    lexicon_matrix,
    token_mask,
    min_share,
):
    mine, heads_mine, head_width, state_width = recurrent_state.shape
    width = heads_mine * head_width
    rows, depth = hidden.shape
    vocab = lexicon_matrix.shape[1]
    row_devices = lax.axis_size("row")
    head_devices = lax.axis_size("head")
    group_devices = head_devices // GROUPS
    columns = group_weight.shape[1]
    entries = columns // GROUPS
    held_rows = 8

    heads = jnp.pad(
        jnp.stack([timestep_bias, decay_log, skip_gain]), ((0, 0), (0, LANES - heads_mine))
    )
    inner_state = jnp.moveaxis(conv_inner_state, 1, 0)
    group_state = jnp.moveaxis(conv_group_state, 1, 0)
    state = recurrent_state.reshape(mine, width, state_width)
    floors = jnp.broadcast_to(min_share[:, None], (mine, LANES))

    kept_arrays = [hidden, norm_gain.reshape(-1, LANES), step_weight.T]
    used_arrays = [group_weight, group_state, conv_group_weight]
    hidden_held, gain_held, step_held, group_part, squares, sent = call(
        functools.partial(group_kernel, len(kept_arrays)),
        [pltpu.VMEM(array.shape, array.dtype) for array in kept_arrays]
        + [
            shape((rows, columns)),
            shape((rows, LANES)),
            shape((head_devices, rows + held_rows, 2 * entries), bf16),
        ],
        [in_hbm(array) for array in kept_arrays + used_arrays],
        [ANY] * 6,
        scratch=[pltpu.VMEM((columns, columns), bf16)]
        + [pltpu.VMEM(array.shape, array.dtype) for array in used_arrays]
        + [
            pltpu.VMEM((2 * rows + 2 * held_rows, columns), f32),
            pltpu.SemaphoreType.DMA((6,)),
        ],
        limit=6,
        cost=2 * MIB,
        out_specs=[VMEM] * 6,
        name="group_projection",
    )
    arrived = lax.all_to_all(sent, "head", 0, 0, tiled=True)
    all_squares = [squares] + [row_send(squares, at) for at in range(1, row_devices)]
    pairs = width // TILE
    early = 2 * (pairs * EARLY_INPUT // 8)
    late = width // LANES - early
    input_held = fetch(
        [(input_weight, "tiles", at, (2, 2 * depth, LANES)) for at in range(0, early, 2)],
        arrived,
        "fetch_input",
    )
    parts = 1
    both, small = call(
        functools.partial(input_kernel, row_devices, len(input_held)),
        [shape((2 * rows, width)), shape((rows, 2 * LANES))],
        all_squares + [hidden_held, gain_held, step_held] + input_held + [in_hbm(input_weight)],
        [VMEM] * (row_devices + 3 + len(input_held)) + [ANY],
        scratch=[
            pltpu.VMEM((2 * rows, 2 * depth), bf16),
            pltpu.VMEM((late, 2 * depth, LANES), bf16),
            pltpu.SemaphoreType.DMA((late * parts,)),
        ],
        limit=late + 6,
        cost=2 * input_weight.size,
        name="input_projection",
    )
    tiles = vocab // TILE
    cuts = [tiles * share // 32 * TILE for share in SHARES]
    spans = [(start, end - start) for start, end in zip([0] + cuts[:-1], cuts)]
    fetched = []

    def lexicon_job(stage):
        start, size = spans[stage]
        return (lexicon_matrix, "columns", start, (depth, size))

    def fetch_lexicon(stage, after, name):
        if not spans[stage][1]:
            return after
        fetched.extend(fetch([lexicon_job(stage)], after, name))
        return fetched[-1]

    packed_width = 2 * width + columns + LANES + 2 * state_width
    packed, held = call(
        pack_kernel,
        [
            shape((row_devices, mine, packed_width + LANES), jnp.int16),
            shape((2, held_rows, 2 * state_width)),
        ],
        [both, group_part, small, arrived],
        [VMEM] * 4,
        scratch=[pltpu.VMEM((rows, 2 * state_width), f32)],
        cost=64 * MIB,
        name="pack_rows",
    )
    pieces = [packed[0]] + [row_send(packed[at], at) for at in range(1, row_devices)]

    *fetched, spread = fetch(
        [lexicon_job(0)],
        packed,
        "fetch_lexicon_0",
        [(head_matrix, (LANES, width))],
    )
    finish = group_devices == 1
    mixer_in, raw, driven, decay, state_input = call(
        functools.partial(state_kernel, finish, row_devices),
        [
            shape((mine, width), bf16 if finish else f32),
            shape((mine, width + columns)),
            shape((mine, width)),
            shape((mine, width)),
            shape((mine, state_width)),
        ],
        pieces + [heads, held, inner_state, conv_inner_weight, state, mixer_gain[None], spread],
        [VMEM] * (row_devices + 7),
        limit=8,
        cost=1000,
        name="state_readout",
    )
    if not finish:
        members = [
            [group * group_devices + at for at in range(group_devices)] for group in range(GROUPS)
        ]
        group_total = lax.psum(jnp.sum(mixer_in * mixer_in, axis=1), "head", axis_index_groups=members)
        group_scale = lax.rsqrt(group_total / (HEADS * HEAD_DIM // GROUPS) + EPSILON)
        mixer_in = (mixer_in * group_scale[:, None] * mixer_gain.astype(f32)[None]).astype(bf16)

    mixer_rows = [mixer_in] + [row_send(mixer_in, at) for at in range(1, row_devices)]
    ahead = fetch_lexicon(1, mixer_in, "fetch_lexicon_1")
    mixed = call(
        functools.partial(output_kernel, row_devices),
        shape((rows, depth)),
        mixer_rows + [output_weight, ahead],
        [VMEM] * (row_devices + 1) + [ANY],
        scratch=[pltpu.VMEM((row_devices, mine, width), f32)],
        cost=1000,
        name="output_projection",
    )
    distance, stage, terms = 1, 2, [mixed]
    while distance < head_devices:
        steps = [distance]
        if distance > 1 and 4 * distance <= head_devices:
            steps = [distance, 2 * distance, 3 * distance]
        mine_now = terms[0]
        if distance > 1:
            mine_now = call(
                encode_kernel, shape((rows, depth + LANES), jnp.int16), terms, [VMEM] * len(terms), name="encode"
            )
        terms = [mine_now] + [xor_permute(mine_now, "head", step) for step in steps]
        if distance > 1 and stage < len(SHARES):
            fetch_lexicon(stage, mine_now, f"fetch_lexicon_{stage}")
            stage += 1
        distance *= 1 + len(steps)
    layer, scores = call(
        functools.partial(lexicon_kernel, len(terms), len(fetched)),
        [pltpu.VMEM((rows, depth), bf16), shape((row_devices, mine, vocab + LANES), jnp.int16)],
        [hidden_held, final_gain[None]] + terms + fetched + [in_hbm(lexicon_matrix)],
        [VMEM] * (2 + len(terms) + len(fetched)) + [ANY],
        scratch=[
            pltpu.VMEM((depth, vocab - cuts[-1]), bf16),
            pltpu.VMEM((2 * rows, depth), bf16),
            pltpu.VMEM((rows, vocab + LANES), f32),
            pltpu.SemaphoreType.DMA((max(1, (vocab - cuts[-1]) // (2 * TILE)),)),
        ],
        limit=16,
        cost=16 * MIB,
        name="lexicon_projection",
    )
    score_rows = [scores[0]] + [row_send(scores[at], at) for at in range(1, row_devices)]
    next_state, next_inner, next_group, layer_out = call(
        update_kernel,
        [
            shape((mine, width, state_width), bf16),
            shape((3, mine, width), bf16),
            shape((3, mine, columns), bf16),
            shape((rows, depth), bf16),
        ],
        [driven, decay, state_input, state, raw, inner_state, group_state, layer, scores],
        [VMEM] * 8 + [ANY],
        scratch=[
            pltpu.VMEM((mine, width, state_width), bf16),
            pltpu.SemaphoreType.DMA((mine, width // min(512, width))),
        ],
        limit=8,
        cost=4 * MIB,
        out_specs=[ANY, VMEM, VMEM, VMEM],
        name="state_update",
    )
    lines = 8 * mine
    shares, share, top = call(
        functools.partial(share_kernel, row_devices),
        [
            shape((lines, vocab * mine // lines + LANES), bf16),
            shape((mine, vocab)),
            shape((mine, LANES)),
        ],
        score_rows + [token_mask],
        [VMEM] * (row_devices + 1),
        scratch=[pltpu.VMEM((lines, vocab * mine // lines + LANES), f32)],
        name="share_of_peak",
    )
    every = lax.all_gather(shares, "head", axis=0)
    next_probs = call(
        probability_kernel,
        shape((mine, vocab), bf16),
        [every, share, top, floors],
        [VMEM] * 4,
        name="probabilities",
    )
    return (
        next_state.reshape(recurrent_state.shape),
        jnp.moveaxis(next_inner, 0, 1),
        jnp.moveaxis(next_group, 0, 1),
        layer_out,
        next_probs,
    )


def solution(mesh):
    in_specs = (
        P(None, "row"),
        P("row"),
        P("row", None, "head"),
        P("row", "head"),
        P("row", "head"),
        P(None, "head"),
        P(None, "head"),
        P("row", None, "head"),
        P("row", None, "head"),
        P("head"),
        P("head"),
        P("head"),
        P("row", "head", None, None),
        P("head"),
        P("head", "row"),
        P("row"),
        P("row", "head"),
        P("row", "head"),
        P("row"),
    )
    out_specs = (
        P("row", "head", None, None),
        P("row", None, "head"),
        P("row", None, "head"),
        P(None, "row"),
        P("row", "head"),
    )
    return jax.shard_map(local, mesh=mesh, in_specs=in_specs, out_specs=out_specs, check_vma=False)
```
